128 devices in a mesh: dp: 16 (over x, z), tensor: 8 (over y, core).
Axes of the slice: x: 4, y: 4, z: 4, core: 2. Of those that a mesh axis runs over, the one named last changes fastest.
Arguments:
- tokens: bfloat16 [2048, 4096], P('dp', 'tensor'), may hold values from -6 to 6
- cotangent: bfloat16 [2048, 4096], P('dp', 'tensor'), may hold values from -6 to 6
- gates: float32 [2048, 2], P('dp'), may hold values from 0.1 to 1
- routes: int32 [2048, 2], P('dp'), may hold values from 0 to 15, all different within a row; in each aligned block of 128 rows (0 to 127, 128 to 255, ...) at most 32 rows name the same one
- dense_gate: bfloat16 [4096, 4096], P(None, 'tensor'), may hold values from -0.125 to 0.125
- dense_up: bfloat16 [4096, 4096], P(None, 'tensor'), may hold values from -0.09375 to 0.09375
- dense_down: bfloat16 [4096, 4096], P('tensor'), may hold values from -0.125 to 0.125
- expert_gate: bfloat16 [16, 4096, 3072], P('dp', None, 'tensor'), may hold values from -0.125 to 0.125
- expert_up: bfloat16 [16, 4096, 3072], P('dp', None, 'tensor'), may hold values from -0.09375 to 0.09375
- expert_down: bfloat16 [16, 3072, 4096], P('dp', 'tensor'), may hold values from -0.15625 to 0.15625
Outputs:
- mixed: bfloat16 [2048, 4096], P('dp', 'tensor')
- token_grad: bfloat16 [2048, 4096], P('dp', 'tensor')
- gate_grad: float32 [2048, 2], P('dp')
The draws below stay inside these ranges and needn't reach their ends.
Inputs may be any that keep to these rules, and one draw needn't show every extreme that they name: `routes`: each token names 2 different experts. Within each aligned block of 128 tokens no expert is named more than 32 times, and in some block some expert is named exactly 32 times; every expert is named somewhere.
All inputs are finite; a program needn't handle non-finite values.
Results may differ from the reference program's by a relative error of at most 0.023.
Values may be sent and summed in bfloat16 or wider, within the bound.
No kernel may reach another device: no remote copies, remote signals or barrier semaphores. Data moves between devices by JAX's collectives and lax.ppermute only.
A program may use at most 128 MiB of HBM per device.

```python
import math
import jax
import jax.numpy as jnp
import numpy as np
from jax import lax

D = 4096
DH = 4096
EH = 3072
TOP = 2
TOK_DEV = 128
TOKENS = 2048
EXPERTS = 16
CAP = 32
N_DP = 16
N_TENSOR = 8


def strengthened(array, key, source, target, parts, factor):
    def block_of(position):
        return (jnp.arange(array.shape[position]) // (array.shape[position] // parts)).reshape((-1,) + (1,) * (array.ndim - 1 - position))

    one_side = jax.random.permutation(key, parts)[block_of(target)]
    second = (block_of(target) + parts // 2) % parts
    return jnp.where((block_of(source) == one_side) | (block_of(source) == second), factor * array, array)


def shard_levels(own_key, dims, pieces, low, high):
    def one(dim, parts):
        heights = jax.random.uniform(jax.random.fold_in(jax.random.fold_in(own_key, 6), dim), (parts,), jnp.float32, low / len(pieces), high / len(pieces))
        return jnp.repeat(jnp.exp(heights), dims[dim] // parts).reshape((-1,) + (1,) * (len(dims) - dim - 1))

    gain = one(*pieces[0])
    for cut in pieces[1:]:
        gain = gain * one(*cut)
    return gain


def shared_out(rng, own, number, rows, count, top, limit, skew):
    ranking = jax.random.permutation(rng, count)
    crowded, common = portions_of(count, rows * top, limit, skew, True), portions_of(count, rows * top, limit, skew, False)
    places = jnp.arange(count)

    def named(lengths, rotation):
        used = int((lengths > 0).sum())
        fixed = max(1, used // 4)
        passed = fixed + (places - fixed + rotation * (used - fixed)) % max(1, count - fixed)
        return jnp.zeros((count,), jnp.int32).at[ranking[jnp.where(places < fixed, places, passed)]].set(jnp.asarray(lengths, jnp.int32))

    lengths = jnp.where(number % 4 == 0, named(crowded, number // 4), named(common, number - number // 4 - 1))
    mixed = jax.random.permutation(jax.random.fold_in(own, 3), count)
    donor, taker = mixed[0:count // 2 * 2:2], mixed[1:count // 2 * 2:2]
    room = jnp.minimum(lengths[donor] - 1, limit - lengths[taker]) // 2
    room = jnp.where((donor == ranking[0]) | (taker == ranking[0]) | (lengths[taker] == 0), 0, jnp.maximum(room, 0))
    passed = jax.random.randint(jax.random.fold_in(own, 4), (count // 2,), 0, 1 << 20) % (room + 1)
    lengths = lengths.at[donor].add(-passed).at[taker].add(passed)
    labels = jnp.searchsorted(jnp.cumsum(lengths), jnp.arange(rows * top), side="right").astype(jnp.int32)
    table = labels.reshape(top, rows).T
    table = table[jax.random.permutation(jax.random.fold_in(own, 1), rows)]
    rotation = jax.random.randint(jax.random.fold_in(own, 2), (rows, 1), 0, top)
    return jnp.take_along_axis(table, (jnp.arange(top)[None, :] + rotation) % top, axis=1)


def portions_of(amount, total, reach, slope, full):
    loads = [(1 << 20) // math.isqrt(grade ** slope) + 1 for grade in range(1, amount + 1)]
    largest = reach if full else min(reach, max(-(-total // amount), total * loads[0] // sum(loads)))
    least = 1 if total - largest >= amount - 1 else 0
    given, rest = [largest] + [least] * (amount - 1), total - largest - least * (amount - 1)
    while rest > 0:
        free = [i for i in range(1, amount) if given[i] < largest] or [i for i in range(1, amount) if given[i] < reach]
        mass, budget = sum([loads[i] for i in free]), rest
        for i in free:
            more = min(reach - given[i], max(1, budget * loads[i] // mass), rest)
            given[i] = given[i] + more
            rest = rest - more
    return np.array(given)


def bell_draw(rng, shape, deviation, most, split=(), held_as=jnp.bfloat16):
    values = deviation * jax.random.normal(rng, shape, jnp.float32)
    if split:
        values = values * shard_levels(rng, shape, split, -0.22, 0.18)
    return jnp.clip(values, -most, most).astype(held_as)


def gaussian_with(key, shape, spread, most, shards, heavy, kind=jnp.bfloat16):
    drawn = spread * jax.random.normal(key, shape, jnp.float32)
    if shards:
        drawn = drawn * shard_levels(key, shape, shards, -0.22, 0.18)
    return jnp.clip(strengthened(drawn, jax.random.fold_in(key, 3), *heavy), -most, most).astype(kind)


def setup_inputs(seed: int = 0) -> dict:
    seeds = jax.random.split(jax.random.key(seed), 11)
    tokens = bell_draw(seeds[0], (TOKENS, D), 1.0, 6.0, ((0, 16), (1, 8)))
    cotangent = bell_draw(seeds[1], (TOKENS, D), 1.0, 6.0, ((0, 16), (1, 8)))
    gates = jnp.clip(0.1 + 0.9 * jax.random.uniform(seeds[2], (TOKENS, TOP), jnp.float32) ** shard_levels(seeds[2], (TOKENS, TOP), ((0, 16),), -0.2, 0.2), 0.1, 1.0)
    routes_keys = jax.random.split(jax.random.fold_in(seeds[3], 1), TOKENS // TOK_DEV)
    routes_turns = jax.random.permutation(jax.random.fold_in(seeds[3], 3), TOKENS // TOK_DEV)
    routes = jax.vmap(lambda own, number: shared_out(jax.random.fold_in(seeds[3], 2), own, number, TOK_DEV, EXPERTS, TOP, CAP, 2))(routes_keys, routes_turns).reshape((TOKENS, TOP))
    dense_gate = gaussian_with(seeds[4], (D, DH), D ** -0.5, 0.125, ((1, 8),), (1, 0, 8, 2.0))
    dense_up = bell_draw(seeds[5], (D, DH), D ** -0.5, 0.09375, ((1, 8),))
    dense_down = gaussian_with(seeds[6], (DH, D), DH ** -0.5, 0.125, ((0, 8),), (0, 1, 8, 2.0))
    expert_gate = gaussian_with(seeds[7], (EXPERTS, D, EH), D ** -0.5, 0.125, ((0, 16), (2, 8)), (2, 1, 8, 2.0))
    expert_up = bell_draw(seeds[8], (EXPERTS, D, EH), D ** -0.5, 0.09375, ((0, 16), (2, 8)))
    expert_down = gaussian_with(seeds[9], (EXPERTS, EH, D), EH ** -0.5, 0.15625, ((0, 16), (1, 8)), (1, 2, 8, 2.0))
    return {"tokens": tokens, "cotangent": cotangent, "gates": gates, "routes": routes, "dense_gate": dense_gate, "dense_up": dense_up, "dense_down": dense_down, "expert_gate": expert_gate, "expert_up": expert_up, "expert_down": expert_down}


def rounded(value):
    return lax.optimization_barrier(value.astype(jnp.bfloat16)).astype(jnp.float32)


def gated_pass(rows, row_grads, weight_gate, weight_up, weight_down):
    block_width = weight_gate.shape[1] // N_TENSOR
    out_sum = jnp.zeros((rows.shape[0], weight_down.shape[1]), jnp.float32)
    grad_sum = jnp.zeros((rows.shape[0], weight_gate.shape[0]), jnp.float32)
    for block in range(N_TENSOR):
        low = block * block_width
        part_gate = weight_gate[:, low:low + block_width]
        part_up = weight_up[:, low:low + block_width]
        part_down = weight_down[low:low + block_width, :]
        gate_pre = jnp.dot(rows, part_gate, preferred_element_type=jnp.float32)
        up_pre = jnp.dot(rows, part_up, preferred_element_type=jnp.float32)
        sigmoid_a = jax.nn.sigmoid(gate_pre)
        activated = gate_pre * sigmoid_a
        hidden = (activated * up_pre).astype(jnp.bfloat16)
        out_sum = out_sum + rounded(jnp.dot(hidden, part_down, preferred_element_type=jnp.float32))
        hidden_grad = jnp.dot(row_grads, part_down.T, preferred_element_type=jnp.float32)
        grad_gate = (hidden_grad * up_pre * sigmoid_a * (1.0 + gate_pre * (1.0 - sigmoid_a))).astype(jnp.bfloat16)
        grad_up = (hidden_grad * activated).astype(jnp.bfloat16)
        term = jnp.dot(grad_gate, part_gate.T, preferred_element_type=jnp.float32)
        term = term + jnp.dot(grad_up, part_up.T, preferred_element_type=jnp.float32)
        grad_sum = grad_sum + rounded(term)
    return out_sum, grad_sum


def block_slots(block_ids):
    flat_ids = block_ids.reshape(-1)
    one_hot = (flat_ids[:, None] == jnp.arange(EXPERTS, dtype=jnp.int32)[None, :]).astype(jnp.int32)
    earlier = jnp.cumsum(one_hot, axis=0) - one_hot
    return jnp.sum(earlier * one_hot, axis=1).astype(jnp.int32)


def reference(tokens, cotangent, gates, routes, dense_gate, dense_up, dense_down, expert_gate, expert_up, expert_down):
    dense_out, dense_grad = gated_pass(tokens, cotangent, dense_gate, dense_up, dense_down)
    block_ids = routes.reshape(N_DP, TOK_DEV * TOP)
    slot_pos = jax.vmap(block_slots)(block_ids)
    block_num = jnp.arange(N_DP, dtype=jnp.int32)[:, None]
    slot_index = (block_ids * (N_DP * CAP) + block_num * CAP + slot_pos).reshape(-1).astype(jnp.int32)
    pair_count = TOKENS * TOP
    slot_table = jnp.full((EXPERTS * N_DP * CAP,), pair_count, jnp.int32)
    slot_table = slot_table.at[slot_index].set(jnp.arange(pair_count, dtype=jnp.int32))
    token_of = jnp.where(slot_table < pair_count, slot_table // TOP, TOKENS).astype(jnp.int32)
    token_ext = jnp.concatenate([tokens, jnp.zeros((1, D), jnp.bfloat16)], axis=0)
    expert_rows = token_ext[token_of].reshape(EXPERTS, N_DP * CAP, D)
    scaled = (gates[:, :, None] * cotangent.astype(jnp.float32)[:, None, :]).astype(jnp.bfloat16)
    scaled_ext = jnp.concatenate([scaled.reshape(pair_count, D), jnp.zeros((1, D), jnp.bfloat16)], axis=0)
    expert_cotan = scaled_ext[slot_table].reshape(EXPERTS, N_DP * CAP, D)

    def one_expert(packed):
        rows, row_grads, weight_gate, weight_up, weight_down = packed
        out_sum, grad_sum = gated_pass(rows, row_grads, weight_gate, weight_up, weight_down)
        return out_sum.astype(jnp.bfloat16), grad_sum.astype(jnp.bfloat16)

    expert_out, expert_grad = lax.map(one_expert, (expert_rows, expert_cotan, expert_gate, expert_up, expert_down))
    pair_out = expert_out.reshape(-1, D)[slot_index].reshape(TOKENS, TOP, D).astype(jnp.float32)
    pair_grad = expert_grad.reshape(-1, D)[slot_index].reshape(TOKENS, TOP, D).astype(jnp.float32)
    mixed = (dense_out + jnp.sum(gates[:, :, None] * pair_out, axis=1)).astype(jnp.bfloat16)
    token_grad = (dense_grad + jnp.sum(pair_grad, axis=1)).astype(jnp.bfloat16)
    gate_grad = jnp.sum(cotangent.astype(jnp.float32)[:, None, :] * pair_out, axis=2)
    return mixed, token_grad, gate_grad
```

```python
import functools

import jax
import jax.numpy as jnp
from jax import lax
from jax.experimental import pallas as pl
from jax.experimental.pallas import tpu as pltpu
from jax.sharding import PartitionSpec as P

F32 = jnp.float32
BF16 = jnp.bfloat16
MIB = 1 << 20
CAPACITY = 32
SIDES = 4


def dot(a, b, contract=((1,), (0,))):
    return lax.dot_general(a, b, (contract, ((), ())), preferred_element_type=F32)


def dot_nt(a, b):
    return dot(a, b, ((1,), (1,)))


def dot_tn(a, b):
    return dot(a, b, ((0,), (0,)))


def gate_terms(a, b):
    s = jax.nn.sigmoid(a)
    act = a * s
    return act, (act * b).astype(BF16), b * s * (1.0 + a * (1.0 - s))


def plan_kernel(routes_ref, gates_ref, cotan_ref, pick_ref, send_ref):
    rows = routes_ref.shape[0]
    slots = pick_ref.shape[1]
    lane = lax.broadcasted_iota(jnp.int32, (rows, 128), 1)
    one = [(routes_ref[:, k : k + 1] == lane).astype(F32) for k in range(2)]
    lower = (
        lax.broadcasted_iota(jnp.int32, (rows, rows), 1)
        < lax.broadcasted_iota(jnp.int32, (rows, rows), 0)
    ).astype(BF16)
    earlier = dot(lower, (one[0] + one[1]).astype(BF16))
    place = lax.broadcasted_iota(jnp.int32, (rows, slots), 1)
    cotan = cotan_ref[...].astype(F32)
    total = None
    for k in range(2):
        pos = jnp.sum(earlier * one[k], axis=1, keepdims=True).astype(jnp.int32)
        slot = routes_ref[:, k : k + 1] * CAPACITY + pos
        pick = (slot == place).astype(BF16)
        pick_ref[k * rows : (k + 1) * rows, :] = pick
        scaled = (gates_ref[:, k : k + 1] * cotan).astype(BF16)
        term = dot_tn(pick, scaled)
        total = term if total is None else total + term
    send_ref[...] = total.astype(BF16)


def rows_kernel(pick_ref, p0, p1, p2, p3, after, send_ref):
    rows = p0.shape[0] // 2
    width = p0.shape[1]
    pick = pick_ref[:rows, :] + pick_ref[rows:, :]
    for d, piece in enumerate((p0, p1, p2, p3)):
        send_ref[:, d * width : (d + 1) * width] = dot_tn(pick, piece[:rows, :]).astype(BF16)


def block_at(offs, i, width):
    return pl.ds(pl.multiple_of(offs[i], 512), width)


def dense_kernel(offs, *refs):
    pieces, (wg, wu, wd), outs = refs[:8], refs[9:12], refs[12:]
    rows = pieces[0].shape[0] // 2
    width = pieces[0].shape[1]
    a = b = g = None
    for i in range(8):
        at = block_at(offs, i, width)
        x, c = pieces[i][:rows, :], pieces[i][rows:, :]
        ta, tb, tg = dot(x, wg[at, :]), dot(x, wu[at, :]), dot_nt(c, wd[:, at])
        a, b, g = (ta, tb, tg) if a is None else (a + ta, b + tb, g + tg)
    act, hidden, slope = gate_terms(a, b)
    da, du = (g * slope).astype(BF16), (g * act).astype(BF16)
    for i in range(8):
        at = block_at(offs, i, width)
        out, d = outs[i // 4], i % 4
        out[:rows, d * width : (d + 1) * width] = dot(hidden, wd[:, at]).astype(BF16)
        out[rows:, d * width : (d + 1) * width] = (
            dot_nt(da, wg[at, :]) + dot_nt(du, wu[at, :])
        ).astype(BF16)


def dense_sum_kernel(mine, got, out_ref, g0, g1, g2, g3):
    rows = out_ref.shape[0]
    width = g0.shape[1]
    out_ref[...] = mine[:rows, :].astype(F32) + got[:rows, :].astype(F32)
    for d, ref in enumerate((g0, g1, g2, g3)):
        at = slice(d * width, (d + 1) * width)
        ref[...] = (mine[rows:, at].astype(F32) + got[rows:, at].astype(F32)).astype(ref.dtype)


def back_kernel(offs, *refs):
    pieces, wd, g_ref = refs[:8], refs[8], refs[9]
    width = pieces[0].shape[1]
    g = None
    for i in range(8):
        term = dot_nt(pieces[i][...], wd[:, block_at(offs, i, width)])
        g = term if g is None else g + term
    g_ref[...] = g


def forth_kernel(offs, xm, xo, g_ref, wg, wu, wd, oo, hid_ref, dadu_ref, ab):
    width = 512
    units = wg.shape[1]
    for i in range(8):
        at = block_at(offs, i, width)
        ref, d = (xm, xo)[i // 4], i % 4
        w = jnp.concatenate([wg[at, :], wu[at, :]], axis=1)
        term = dot(ref[:, d * width : (d + 1) * width], w)
        if i == 0:
            ab[...] = term
        else:
            ab[...] += term
    act, hidden, slope = gate_terms(ab[:, :units], ab[:, units:])
    g = g_ref[...]
    hid_ref[...] = hidden
    dadu_ref[:, :units] = (g * slope).astype(BF16)
    dadu_ref[:, units:] = (g * act).astype(BF16)
    for d in range(4):
        oo[:, d * width : (d + 1) * width] = dot(
            hidden, wd[:, block_at(offs, 4 + d, width)]
        ).astype(BF16)


def out_kernel(offs, hid_ref, wd, om):
    width = 512
    for d in range(4):
        om[:, d * width : (d + 1) * width] = dot(
            hid_ref[...], wd[:, block_at(offs, d, width)]
        ).astype(BF16)


def down_kernel(first, offs, dadu_ref, wg, wu, after, out):
    width = 512
    for d in range(4):
        at = block_at(offs, first + d, width)
        w = jnp.concatenate([wg[at, :], wu[at, :]], axis=1)
        out[:, d * width : (d + 1) * width] = dot_nt(dadu_ref[...], w).astype(BF16)


def add_kernel(mine, got, out):
    out[...] = (mine[...].astype(F32) + got[...].astype(F32)).astype(BF16)


def split_kernel(mine, got, *outs):
    width = outs[0].shape[1]
    for d, ref in enumerate(outs):
        at = slice(d * width, (d + 1) * width)
        ref[...] = (mine[:, at].astype(F32) + got[:, at].astype(F32)).astype(ref.dtype)


def sum_kernel(p0, p1, p2, p3, after, out):
    out[...] = (
        p0[...] + p1[...].astype(F32) + p2[...].astype(F32) + p3[...].astype(F32)
    ).astype(BF16)


def mix_kernel(back, pick, gates, dense, c0, c1, c2, c3, m0, m1, m2, m3, inner_ref):
    rows = gates.shape[0]
    width = 512
    inner = [None, None]
    for d, (cot, out) in enumerate(((c0, m0), (c1, m1), (c2, m2), (c3, m3))):
        cotan = cot[rows:, :].astype(F32)
        y = dot(pick[...], back[:, d * width : (d + 1) * width])
        total = dense[:, d * width : (d + 1) * width]
        for k in range(2):
            yk = y[k * rows : (k + 1) * rows, :]
            total = total + gates[:, k : k + 1] * yk
            term = jnp.sum(cotan * yk, axis=1, keepdims=True)
            inner[k] = term if inner[k] is None else inner[k] + term
        out[...] = total.astype(BF16)
    lane = lax.broadcasted_iota(jnp.int32, (rows, 128), 1)
    inner_ref[...] = jnp.where(lane == 0, inner[0], jnp.where(lane == 1, inner[1], 0.0))


def grad_kernel(back, pick, d0, d1, d2, d3, out):
    rows = out.shape[0]
    z = dot(pick[:rows, :] + pick[rows:, :], back[...])
    dense = d0[...] + d1[...].astype(F32) + d2[...].astype(F32) + d3[...].astype(F32)
    out[...] = (dense + z).astype(BF16)


def call(kernel, outs, limit, flops, prefetch, args, name, after=None, scratch=()):
    vmem = pl.BlockSpec(memory_space=pltpu.VMEM)
    smem = pl.BlockSpec(memory_space=pltpu.SMEM)
    moved = sum(a.size * a.dtype.itemsize for a in args)
    return pl.pallas_call(
        kernel,
        out_shape=[jax.ShapeDtypeStruct(*o) for o in outs],
        in_specs=[
            smem if i < prefetch else pl.BlockSpec(memory_space=pl.ANY) if i == after else vmem
            for i in range(len(args))
        ],
        out_specs=[vmem] * len(outs),
        compiler_params=pltpu.CompilerParams(vmem_limit_bytes=limit * MIB),
        cost_estimate=pl.CostEstimate(flops=flops, bytes_accessed=moved, transcendentals=0),
        scratch_shapes=list(scratch),
        name=name,
    )(*args)


def local(
    tokens,
    cotangent,
    gates,
    routes,
    dense_gate,
    dense_up,
    dense_down,
    expert_gate,
    expert_up,
    expert_down,
):
    devices = lax.axis_size("tensor")
    rows, width = tokens.shape
    experts = lax.axis_size("dp")
    slots = experts * CAPACITY
    half = SIDES * width
    hidden = expert_gate.shape[2]
    dense_hidden = dense_gate.shape[1]
    me = lax.axis_index("tensor")
    chip, core = me // 2, me % 2

    def along(v, d):
        return lax.ppermute(
            v, "tensor", [(i, (i + 2 * d) % devices) for i in range(devices)]
        )

    def swap(v):
        return lax.ppermute(v, "tensor", [(i, i ^ 1) for i in range(devices)])

    def spread(v):
        return lax.all_to_all(v, "dp", split_axis=0, concat_axis=0, tiled=True)

    steps = jnp.arange(SIDES, dtype=jnp.int32)
    chips = lax.rem(chip + SIDES - steps, SIDES)
    offs = jnp.concatenate([2 * chips + core, 2 * chips + 1 - core]) * width

    wg, wu, wd = expert_gate[0], expert_up[0], expert_down[0]
    both = jnp.concatenate([tokens, cotangent], axis=0)
    own = [both, along(both, 1), along(both, 2), along(both, 3)]
    pick, grads_send = call(
        plan_kernel,
        [((2 * rows, slots), BF16), ((slots, width), BF16)],
        16,
        2 * 2 * rows * slots * width,
        0,
        (routes, gates, cotangent),
        "plan",
    )
    got_grads = spread(grads_send)
    other = [swap(v) for v in own]
    (rows_send,) = call(
        rows_kernel,
        [((slots, half), BF16)],
        12,
        2 * rows * slots * half,
        0,
        (pick, *own, got_grads),
        "rows",
        after=5,
    )
    got_rows = spread(rows_send)
    grads_own = [got_grads] + [along(got_grads, d) for d in (1, 2, 3)]
    dense_m, dense_o = call(
        dense_kernel,
        [((2 * rows, half), BF16)] * 2,
        28,
        12 * rows * dense_hidden * half * 2,
        1,
        (offs, *own, *other, rows_send, dense_gate, dense_up, dense_down),
        "dense",
        after=9,
    )
    dense_out, *dense_part = call(
        dense_sum_kernel,
        [((rows, half), F32), ((rows, width), F32)] + [((rows, width), BF16)] * 3,
        12,
        2 * rows * half,
        0,
        (dense_m, swap(dense_o)),
        "dense_sum",
    )
    dense_got = [dense_part[0]] + [along(dense_part[d], SIDES - d) for d in (1, 2, 3)]
    grads_other = [swap(v) for v in grads_own]
    (g,) = call(
        back_kernel,
        [((slots, hidden), F32)],
        16,
        2 * slots * hidden * half * 2,
        1,
        (offs, *grads_own, *grads_other, wd),
        "back",
    )
    got_rows, g, dense_out, dense_got = lax.optimization_barrier(
        (got_rows, g, dense_out, dense_got)
    )
    rows_other = swap(got_rows)
    out_o, hid, dadu = call(
        forth_kernel,
        [((slots, half), BF16), ((slots, hidden), BF16), ((slots, 2 * hidden), BF16)],
        28,
        5 * slots * hidden * half * 2,
        1,
        (offs, got_rows, rows_other, g, wg, wu, wd),
        "forth",
        scratch=[pltpu.VMEM((slots, 2 * hidden), F32)],
    )
    out_got = swap(out_o)
    (out_m,) = call(
        out_kernel,
        [((slots, half), BF16)],
        12,
        2 * slots * hidden * half,
        1,
        (offs, hid, wd),
        "out",
    )
    (grad_o,) = call(
        functools.partial(down_kernel, 4),
        [((slots, half), BF16)],
        16,
        4 * slots * hidden * half,
        1,
        (offs, dadu, wg, wu, out_m),
        "down_o",
        after=4,
    )
    grad_got = swap(grad_o)
    (out_chip,) = call(
        add_kernel,
        [((slots, half), BF16)],
        12,
        slots * half,
        0,
        (out_m, out_got),
        "add",
    )
    out_back = spread(out_chip)
    (grad_m,) = call(
        functools.partial(down_kernel, 0),
        [((slots, half), BF16)],
        16,
        4 * slots * hidden * half,
        1,
        (offs, dadu, wg, wu, grad_o),
        "down_m",
        after=4,
    )
    grad_part = call(
        split_kernel,
        [((slots, width), F32)] + [((slots, width), BF16)] * 3,
        16,
        slots * half,
        0,
        (grad_m, grad_got),
        "split",
    )
    grad_all = [grad_part[0]] + [along(grad_part[d], SIDES - d) for d in (1, 2, 3)]
    m0, m1, m2, m3, inner = call(
        mix_kernel,
        [((rows, width), BF16)] * 4 + [((rows, 128), F32)],
        16,
        4 * rows * slots * half,
        0,
        (out_back, pick, gates, dense_out, *own),
        "mix",
    )
    (grad_sum,) = call(
        sum_kernel,
        [((slots, width), BF16)],
        12,
        3 * slots * width,
        0,
        (*grad_all, inner),
        "sum",
        after=4,
    )
    grad_back = spread(grad_sum)
    mixed = m0.astype(F32)
    for d, part in ((1, m1), (2, m2), (3, m3)):
        mixed = mixed + along(part, SIDES - d).astype(F32)
    inner = inner[:, :2]
    inner = inner + swap(inner)
    gate_grad = inner + along(inner, 1) + along(inner, 2) + along(inner, 3)
    (token_grad,) = call(
        grad_kernel,
        [((rows, width), BF16)],
        12,
        2 * rows * slots * width,
        0,
        (grad_back, pick, *dense_got),
        "grad",
    )
    return (mixed.astype(BF16), token_grad, gate_grad)


def solution(mesh):
    in_specs = (
        P("dp", "tensor"),
        P("dp", "tensor"),
        P("dp", None),
        P("dp", None),
        P(None, "tensor"),
        P(None, "tensor"),
        P("tensor", None),
        P("dp", None, "tensor"),
        P("dp", None, "tensor"),
        P("dp", "tensor", None),
    )
    out_specs = (P("dp", "tensor"), P("dp", "tensor"), P("dp", None))
    return jax.shard_map(local, mesh=mesh, in_specs=in_specs, out_specs=out_specs, check_vma=False)
```

```python
import functools

import jax
import jax.numpy as jnp
from jax import lax
from jax.experimental import pallas as pl
from jax.experimental.pallas import tpu as pltpu
from jax.sharding import PartitionSpec as P

F32 = jnp.float32
BF16 = jnp.bfloat16
MIB = 1 << 20
CAPACITY = 32
SIDES = 4


def dot(a, b, contract=((1,), (0,))):
    return lax.dot_general(a, b, (contract, ((), ())), preferred_element_type=F32)


def dot_nt(a, b):
    return dot(a, b, ((1,), (1,)))


def dot_tn(a, b):
    return dot(a, b, ((0,), (0,)))


def gate_terms(a, b):
    s = jax.nn.sigmoid(a)
    act = a * s
    return act, (act * b).astype(BF16), b * s * (1.0 + a * (1.0 - s))


def plan_kernel(routes_ref, gates_ref, cotan_ref, pick_ref, send_ref):
    rows = routes_ref.shape[0]
    slots = pick_ref.shape[1]
    lane = lax.broadcasted_iota(jnp.int32, (rows, 128), 1)
    one = [(routes_ref[:, k : k + 1] == lane).astype(F32) for k in range(2)]
    lower = (
        lax.broadcasted_iota(jnp.int32, (rows, rows), 1)
        < lax.broadcasted_iota(jnp.int32, (rows, rows), 0)
    ).astype(BF16)
    earlier = dot(lower, (one[0] + one[1]).astype(BF16))
    place = lax.broadcasted_iota(jnp.int32, (rows, slots), 1)
    cotan = cotan_ref[...].astype(F32)
    total = None
    for k in range(2):
        pos = jnp.sum(earlier * one[k], axis=1, keepdims=True).astype(jnp.int32)
        slot = routes_ref[:, k : k + 1] * CAPACITY + pos
        pick = (slot == place).astype(BF16)
        pick_ref[k * rows : (k + 1) * rows, :] = pick
        scaled = (gates_ref[:, k : k + 1] * cotan).astype(BF16)
        term = dot_tn(pick, scaled)
        total = term if total is None else total + term
    send_ref[...] = total.astype(BF16)


def rows_kernel(pick_ref, p0, p1, p2, p3, after, send_ref, pack_ref):
    rows = p0.shape[0] // 2
    width = p0.shape[1]
    pick = pick_ref[:rows, :] + pick_ref[rows:, :]
    for d, piece in enumerate((p0, p1, p2, p3)):
        pack_ref[d] = piece[...]
        send_ref[:, d * width : (d + 1) * width] = dot_tn(pick, piece[:rows, :]).astype(BF16)


def starts(width):
    me = lax.axis_index("tensor")
    chip, core = me // 2, lax.rem(me, 2)
    chips = [lax.rem(chip + SIDES - d, SIDES) for d in range(SIDES)]
    mine = [pl.multiple_of((2 * c + core) * width, width) for c in chips]
    other = [pl.multiple_of((2 * c + 1 - core) * width, width) for c in chips]
    return mine + other


class Loads:
    def __init__(self, sems):
        self.sems = sems
        self.count = 0

    def __call__(self, src, dst):
        copy = pltpu.make_async_copy(src, dst, self.sems.at[self.count])
        copy.start()
        self.count += 1
        return copy


def wait(copies):
    for copy in copies:
        copy.wait()


def dense_kernel(*refs):
    sides, (wg, wu, wd), outs = refs[:2], refs[2:5], refs[5:7]
    xs, ws, vs, sems = refs[7:]
    rows = xs.shape[1] // 2
    width = xs.shape[2]
    units = wg.shape[1]
    load = Loads(sems)
    copies = []
    for i, at in enumerate(starts(width)):
        copies.append(
            [
                load(sides[i // 4].at[i % 4], xs.at[i]),
                load(wg.at[pl.ds(at, width), :], ws.at[i, :, pl.ds(0, units)]),
                load(wu.at[pl.ds(at, width), :], ws.at[i, :, pl.ds(units, units)]),
                load(wd.at[:, pl.ds(at, width)], vs.at[i]),
            ]
        )
    ab = g = None
    for i in range(8):
        wait(copies[i])
        tab = dot(xs[i, :rows, :], ws[i])
        tg = dot_nt(xs[i, rows:, :], vs[i])
        ab, g = (tab, tg) if ab is None else (ab + tab, g + tg)
    act, hidden, slope = gate_terms(ab[:, :units], ab[:, units:])
    dadu = jnp.concatenate([(g * slope).astype(BF16), (g * act).astype(BF16)], axis=1)
    for i in range(8):
        out, d = outs[i // 4], i % 4
        out[:rows, d * width : (d + 1) * width] = dot(hidden, vs[i]).astype(BF16)
        out[rows:, d * width : (d + 1) * width] = dot_nt(dadu, ws[i]).astype(BF16)


def dense_sum_kernel(mine, got, out_ref, g0, g1, g2, g3):
    rows = out_ref.shape[0]
    width = g0.shape[1]
    out_ref[...] = (mine[:rows, :].astype(F32) + got[:rows, :].astype(F32)).astype(BF16)
    for d, ref in enumerate((g0, g1, g2, g3)):
        at = slice(d * width, (d + 1) * width)
        ref[...] = (mine[rows:, at].astype(F32) + got[rows:, at].astype(F32)).astype(ref.dtype)


def back_kernel(*refs):
    pieces, wd, g_ref, xs, vs, sems = refs[:8], refs[8], *refs[10:]
    width = pieces[0].shape[1]
    load = Loads(sems)
    copies = [
        [load(pieces[i], xs.at[i]), load(wd.at[:, pl.ds(at, width)], vs.at[i])]
        for i, at in enumerate(starts(width))
    ]
    for i in range(8):
        wait(copies[i])
        term = dot_nt(xs[i], vs[i])
        if i == 0:
            g_ref[...] = term
        else:
            g_ref[...] += term


def half_kernel(side, x, wg, wu, ab, xs, ws, sems):
    width = xs.shape[2]
    units = wg.shape[1]
    load = Loads(sems)
    at = starts(width)[4 * side :]
    copies = [
        [
            load(x.at[:, pl.ds(d * width, width)], xs.at[d]),
            load(wg.at[pl.ds(at[d], width), :], ws.at[d, :, pl.ds(0, units)]),
            load(wu.at[pl.ds(at[d], width), :], ws.at[d, :, pl.ds(units, units)]),
        ]
        for d in range(4)
    ]
    for d in range(4):
        wait(copies[d])
        term = dot(xs[d], ws[d])
        if d == 0 and side == 0:
            ab[...] = term
        else:
            ab[...] += term


def forth_kernel(x, part, g_ref, wg, wu, wd, a1, a2, a3, oo, hid_ref, dadu_ref, ab, xs, ws, vs, gs, sems):
    width = xs.shape[2]
    units = wg.shape[1]
    load = Loads(sems)
    at = starts(width)
    first = load(part, ab)
    more = [load(wd.at[:, pl.ds(at[4 + d], width)], vs.at[d]) for d in range(4)]
    copy_g = load(g_ref, gs)
    first.wait()
    half_kernel(1, x, wg, wu, ab, xs, ws, sems.at[pl.ds(6, 12)])
    act, hidden, slope = gate_terms(ab[:, :units], ab[:, units:])
    copy_g.wait()
    g = gs[...]
    hid_ref[...] = hidden
    dadu_ref[:, :units] = (g * slope).astype(BF16)
    dadu_ref[:, units:] = (g * act).astype(BF16)
    for d in range(4):
        more[d].wait()
        oo[:, d * width : (d + 1) * width] = dot(hidden, vs[d]).astype(BF16)


def cross_kernel(hid_ref, dadu_ref, wg, wu, wd, om, ro, ws, vs, sems):
    width = ws.shape[1]
    units = wg.shape[1]
    load = Loads(sems)
    at = starts(width)
    copies = [
        [
            load(wg.at[pl.ds(at[4 + d], width), :], ws.at[d, :, pl.ds(0, units)]),
            load(wu.at[pl.ds(at[4 + d], width), :], ws.at[d, :, pl.ds(units, units)]),
        ]
        for d in range(4)
    ]
    more = [load(wd.at[:, pl.ds(at[d], width)], vs.at[d]) for d in range(4)]
    for d in range(4):
        wait(copies[d])
        ro[:, d * width : (d + 1) * width] = dot_nt(dadu_ref[...], ws[d]).astype(BF16)
    for d in range(4):
        more[d].wait()
        om[:, d * width : (d + 1) * width] = dot(hid_ref[...], vs[d]).astype(BF16)


def down_kernel(dadu_ref, wg, wu, got, *refs):
    outs, (ws, gs, sems) = refs[:SIDES], refs[SIDES:]
    width = ws.shape[1]
    units = wg.shape[1]
    load = Loads(sems)
    at = starts(width)
    copies = [
        [
            load(wg.at[pl.ds(at[d], width), :], ws.at[d, :, pl.ds(0, units)]),
            load(wu.at[pl.ds(at[d], width), :], ws.at[d, :, pl.ds(units, units)]),
            load(got.at[:, pl.ds(d * width, width)], gs.at[d]),
        ]
        for d in range(SIDES)
    ]
    for d in range(SIDES):
        wait(copies[d])
        outs[d][...] = (dot_nt(dadu_ref[...], ws[d]) + gs[d].astype(F32)).astype(BF16)


def add_kernel(mine, got, out):
    out[...] = (mine[...].astype(F32) + got[...].astype(F32)).astype(BF16)


def sum_kernel(p0, p1, p2, p3, after, out):
    out[...] = (
        p0[...].astype(F32)
        + p1[...].astype(F32)
        + p2[...].astype(F32)
        + p3[...].astype(F32)
    ).astype(BF16)


def mix_kernel(back, pick, gates, dense, pack, m0, m1, m2, m3, inner_ref):
    rows = gates.shape[0]
    width = pack.shape[2]
    inner = [None, None]
    for d, out in enumerate((m0, m1, m2, m3)):
        cotan = pack[d, rows:, :].astype(F32)
        y = dot(pick[...], back[:, d * width : (d + 1) * width])
        total = dense[:, d * width : (d + 1) * width].astype(F32)
        for k in range(2):
            yk = y[k * rows : (k + 1) * rows, :]
            total = total + gates[:, k : k + 1] * yk
            term = jnp.sum(cotan * yk, axis=1, keepdims=True)
            inner[k] = term if inner[k] is None else inner[k] + term
        out[...] = total.astype(BF16)
    lane = lax.broadcasted_iota(jnp.int32, (rows, 128), 1)
    inner_ref[...] = jnp.where(lane == 0, inner[0], jnp.where(lane == 1, inner[1], 0.0))


def grad_kernel(back, pick, d0, d1, d2, d3, out):
    rows = out.shape[0]
    z = dot(pick[:rows, :] + pick[rows:, :], back[...])
    dense = d0[...].astype(F32) + d1[...].astype(F32)
    dense = dense + d2[...].astype(F32) + d3[...].astype(F32)
    out[...] = (dense + z).astype(BF16)


def call(kernel, outs, limit, flops, args, name, far_args=(), scratch=()):
    vmem = pl.BlockSpec(memory_space=pltpu.VMEM)
    far = pl.BlockSpec(memory_space=pl.ANY)
    moved = sum(a.size * a.dtype.itemsize for a in args)
    return pl.pallas_call(
        kernel,
        out_shape=[jax.ShapeDtypeStruct(*o) for o in outs],
        in_specs=[far if i in far_args else vmem for i in range(len(args))],
        out_specs=[vmem] * len(outs),
        compiler_params=pltpu.CompilerParams(vmem_limit_bytes=limit * MIB),
        cost_estimate=pl.CostEstimate(flops=flops, bytes_accessed=moved, transcendentals=0),
        scratch_shapes=list(scratch),
        name=name,
    )(*args)


def local(
    tokens,
    cotangent,
    gates,
    routes,
    dense_gate,
    dense_up,
    dense_down,
    expert_gate,
    expert_up,
    expert_down,
):
    devices = lax.axis_size("tensor")
    rows, width = tokens.shape
    experts = lax.axis_size("dp")
    slots = experts * CAPACITY
    half = SIDES * width
    hidden = expert_gate.shape[2]
    dense_hidden = dense_gate.shape[1]

    def along(v, d):
        return lax.ppermute(
            v, "tensor", [(i, (i + 2 * d) % devices) for i in range(devices)]
        )

    def swap(v):
        return lax.ppermute(v, "tensor", [(i, i ^ 1) for i in range(devices)])

    def spread(v):
        return lax.all_to_all(v, "dp", split_axis=0, concat_axis=0, tiled=True)

    def pin(v):
        return pltpu.with_memory_space_constraint(v, pltpu.HBM)

    wg, wu, wd = pin(expert_gate[0]), pin(expert_up[0]), pin(expert_down[0])
    both = jnp.concatenate([tokens, cotangent], axis=0)
    own = [both] + [along(both, d) for d in (1, 2, 3)]
    sems = pltpu.SemaphoreType.DMA
    pick, grads_send = call(
        plan_kernel,
        [((2 * rows, slots), BF16), ((slots, width), BF16)],
        12,
        2 * 2 * rows * slots * width,
        (routes, gates, cotangent),
        "plan",
    )
    got_grads, own = lax.optimization_barrier((spread(grads_send), own))
    rows_send, pack = call(
        rows_kernel,
        [((slots, half), BF16), ((SIDES, 2 * rows, width), BF16)],
        12,
        2 * rows * slots * half,
        (pick, *own, got_grads),
        "rows",
        far_args=(5,),
    )
    got_rows = spread(rows_send)
    grads_own = [got_grads] + [along(got_grads, d) for d in (1, 2, 3)]
    grads_other = [swap(got_grads)]
    dense_m, dense_o = call(
        dense_kernel,
        [((2 * rows, half), BF16)] * 2,
        24,
        12 * rows * dense_hidden * half * 2,
        (pack, swap(pack), pin(dense_gate), pin(dense_up), pin(dense_down)),
        "dense",
        far_args=range(5),
        scratch=[
            pltpu.VMEM((8, 2 * rows, width), BF16),
            pltpu.VMEM((8, width, 2 * dense_hidden), BF16),
            pltpu.VMEM((8, dense_hidden, width), BF16),
            sems((32,)),
        ],
    )
    grads_own[1:], dense_m = lax.optimization_barrier((grads_own[1:], dense_m))
    grads_other += [swap(v) for v in grads_own[1:]]
    dense_out, *dense_part = call(
        dense_sum_kernel,
        [((rows, half), BF16)] + [((rows, width), BF16)] * SIDES,
        12,
        2 * rows * half,
        (dense_m, swap(dense_o)),
        "dense_sum",
    )
    dense_got = [dense_part[0]] + [along(dense_part[d], SIDES - d) for d in (1, 2, 3)]
    (g,) = call(
        back_kernel,
        [((slots, hidden), F32)],
        16,
        2 * slots * hidden * half * 2,
        (*grads_own, *grads_other, wd, dense_part[0]),
        "back",
        far_args=range(10),
        scratch=[
            pltpu.VMEM((8, slots, width), BF16),
            pltpu.VMEM((8, hidden, width), BF16),
            sems((16,)),
        ],
    )
    got_rows, g, dense_m = lax.optimization_barrier((got_rows, g, dense_m))
    rows_other = swap(got_rows)
    half_scratch = [pltpu.VMEM((4, slots, width), BF16), pltpu.VMEM((4, width, 2 * hidden), BF16)]
    (part,) = call(
        functools.partial(half_kernel, 0),
        [((slots, 2 * hidden), F32)],
        16,
        4 * slots * hidden * half,
        (got_rows, wg, wu),
        "half",
        far_args=(0, 1, 2),
        scratch=[*half_scratch, sems((12,))],
    )
    out_o, hid, dadu = call(
        forth_kernel,
        [((slots, half), BF16), ((slots, hidden), BF16), ((slots, 2 * hidden), BF16)],
        24,
        6 * slots * hidden * half,
        (rows_other, part, g, wg, wu, wd, *dense_got[1:]),
        "forth",
        far_args=range(9),
        scratch=[
            pltpu.VMEM((slots, 2 * hidden), F32),
            *half_scratch,
            pltpu.VMEM((4, hidden, width), BF16),
            pltpu.VMEM((slots, hidden), F32),
            sems((18,)),
        ],
    )
    out_got = swap(out_o)
    out_m, grad_o = call(
        cross_kernel,
        [((slots, half), BF16)] * 2,
        20,
        6 * slots * hidden * half,
        (hid, dadu, wg, wu, wd),
        "cross",
        far_args=range(2, 5),
        scratch=[half_scratch[1], pltpu.VMEM((4, hidden, width), BF16), sems((12,))],
    )
    grad_got = swap(grad_o)
    (out_chip,) = call(
        add_kernel,
        [((slots, half), BF16)],
        12,
        slots * half,
        (out_m, out_got),
        "add",
    )
    out_back = spread(out_chip)
    grad_part = call(
        down_kernel,
        [((slots, width), BF16)] * SIDES,
        20,
        4 * slots * hidden * half,
        (dadu, wg, wu, grad_got),
        "down",
        far_args=(1, 2, 3),
        scratch=[half_scratch[1], pltpu.VMEM((SIDES, slots, width), BF16), sems((12,))],
    )
    grad_all = [grad_part[0]] + [along(grad_part[d], SIDES - d) for d in (1, 2, 3)]
    m0, m1, m2, m3, inner = call(
        mix_kernel,
        [((rows, width), BF16)] * 4 + [((rows, 128), F32)],
        16,
        4 * rows * slots * half,
        (out_back, pick, gates, dense_out, pack),
        "mix",
    )
    (grad_sum,) = call(
        sum_kernel,
        [((slots, width), BF16)],
        12,
        3 * slots * width,
        (*grad_all, inner),
        "sum",
        far_args=(4,),
    )
    grad_back = spread(grad_sum)
    mixed = m0.astype(F32)
    for d, part in ((1, m1), (2, m2), (3, m3)):
        mixed = mixed + along(part, SIDES - d).astype(F32)
    inner = inner[:, :2]
    inner = inner + swap(inner)
    gate_grad = inner + along(inner, 1) + along(inner, 2) + along(inner, 3)
    (token_grad,) = call(
        grad_kernel,
        [((rows, width), BF16)],
        12,
        2 * rows * slots * width,
        (grad_back, pick, *dense_got),
        "grad",
    )
    return (mixed.astype(BF16), token_grad, gate_grad)


def solution(mesh):
    in_specs = (
        P("dp", "tensor"),
        P("dp", "tensor"),
        P("dp", None),
        P("dp", None),
        P(None, "tensor"),
        P(None, "tensor"),
        P("tensor", None),
        P("dp", None, "tensor"),
        P("dp", None, "tensor"),
        P("dp", "tensor", None),
    )
    out_specs = (P("dp", "tensor"), P("dp", "tensor"), P("dp", None))
    return jax.shard_map(local, mesh=mesh, in_specs=in_specs, out_specs=out_specs, check_vma=False)
```

```python
import functools

import jax
import jax.numpy as jnp
from jax import lax
from jax.experimental import pallas as pl
from jax.experimental.pallas import tpu as pltpu
from jax.sharding import PartitionSpec as P

F32 = jnp.float32
BF16 = jnp.bfloat16
MIB = 1 << 20
CAPACITY = 32
SIDES = 4


def dot(a, b, contract=((1,), (0,))):
    return lax.dot_general(a, b, (contract, ((), ())), preferred_element_type=F32)


def dot_nt(a, b):
    return dot(a, b, ((1,), (1,)))


def dot_tn(a, b):
    return dot(a, b, ((0,), (0,)))


def gate_terms(a, b):
    s = jax.nn.sigmoid(a)
    act = a * s
    return act, (act * b).astype(BF16), b * s * (1.0 + a * (1.0 - s))


def column(ref, k):
    rows = ref.shape[1]
    eye = lax.broadcasted_iota(jnp.int32, (rows, rows), 0) == lax.broadcasted_iota(
        jnp.int32, (rows, rows), 1
    )
    return jnp.sum(jnp.where(eye, ref[k : k + 1, :].astype(F32), 0.0), axis=1, keepdims=True)


def plan_kernel(routes, gates, tokens, cotangent, pick_ref, send_ref, both_ref, *scratch):
    routes_ref, gates_ref, sems = scratch
    rows = tokens.shape[0]
    slots = pick_ref.shape[1]
    load = Loads(sems)
    first = load(routes, routes_ref)
    copies = [
        load(gates, gates_ref),
        load(cotangent, both_ref.at[pl.ds(rows, rows), :]),
        load(tokens, both_ref.at[pl.ds(0, rows), :]),
    ]
    first.wait()
    lane = lax.broadcasted_iota(jnp.int32, (rows, 128), 1)
    route = [column(routes_ref, k).astype(jnp.int32) for k in range(2)]
    one = [(route[k] == lane).astype(F32) for k in range(2)]
    lower = (
        lax.broadcasted_iota(jnp.int32, (rows, rows), 1)
        < lax.broadcasted_iota(jnp.int32, (rows, rows), 0)
    ).astype(BF16)
    earlier = dot(lower, (one[0] + one[1]).astype(BF16))
    place = lax.broadcasted_iota(jnp.int32, (rows, slots), 1)
    wait(copies)
    cotan = both_ref[rows:, :].astype(F32)
    total = None
    for k in range(2):
        pos = jnp.sum(earlier * one[k], axis=1, keepdims=True).astype(jnp.int32)
        slot = route[k] * CAPACITY + pos
        pick = (slot == place).astype(BF16)
        pick_ref[k * rows : (k + 1) * rows, :] = pick
        scaled = (column(gates_ref, k) * cotan).astype(BF16)
        term = dot_tn(pick, scaled)
        total = term if total is None else total + term
    send_ref[...] = total.astype(BF16)


def rows_kernel(pick_ref, p0, p1, p2, p3, after, send_ref, pack_ref, out, sems):
    rows = p0.shape[0] // 2
    width = p0.shape[1]
    load = Loads(sems)
    pick = pick_ref[:rows, :] + pick_ref[rows:, :]
    copies = []
    for d, piece in enumerate((p0, p1, p2, p3)):
        at = pl.ds(d * width, width)
        out[:, at] = dot_tn(pick, piece[:rows, :]).astype(BF16)
        copies.append(load(out.at[:, at], send_ref.at[:, at]))
        pack_ref[d] = piece[...]
    wait(copies)


def starts(width):
    me = lax.axis_index("tensor")
    chip, core = me // 2, lax.rem(me, 2)
    chips = [lax.rem(chip + SIDES - d, SIDES) for d in range(SIDES)]
    mine = [pl.multiple_of((2 * c + core) * width, width) for c in chips]
    other = [pl.multiple_of((2 * c + 1 - core) * width, width) for c in chips]
    return mine + other


class Loads:
    def __init__(self, sems):
        self.sems = sems
        self.count = 0

    def __call__(self, src, dst):
        copy = pltpu.make_async_copy(src, dst, self.sems.at[self.count])
        copy.start()
        self.count += 1
        return copy


def wait(copies):
    for copy in copies:
        copy.wait()


def dense_kernel(*refs):
    sides, (wg, wu, wd), outs = refs[:2], refs[2:5], refs[5:7]
    xs, ws, vs, sems = refs[7:]
    rows = xs.shape[1] // 2
    width = xs.shape[2]
    units = wg.shape[1]
    load = Loads(sems)
    copies = []
    for i, at in enumerate(starts(width)):
        copies.append(
            [
                load(sides[i // 4].at[i % 4], xs.at[i]),
                load(wg.at[pl.ds(at, width), :], ws.at[i, :, pl.ds(0, units)]),
                load(wu.at[pl.ds(at, width), :], ws.at[i, :, pl.ds(units, units)]),
                load(wd.at[:, pl.ds(at, width)], vs.at[i]),
            ]
        )
    ab = g = None
    for i in range(8):
        wait(copies[i])
        tab = dot(xs[i, :rows, :], ws[i])
        tg = dot_nt(xs[i, rows:, :], vs[i])
        ab, g = (tab, tg) if ab is None else (ab + tab, g + tg)
    act, hidden, slope = gate_terms(ab[:, :units], ab[:, units:])
    dadu = jnp.concatenate([(g * slope).astype(BF16), (g * act).astype(BF16)], axis=1)
    for i in range(8):
        out, d = outs[i // 4], i % 4
        out[:rows, d * width : (d + 1) * width] = dot(hidden, vs[i]).astype(BF16)
        out[rows:, d * width : (d + 1) * width] = dot_nt(dadu, ws[i]).astype(BF16)


def dense_sum_kernel(mine, got, out_ref, g0, g1, g2, g3):
    rows = out_ref.shape[0]
    width = g0.shape[1]
    out_ref[...] = (mine[:rows, :].astype(F32) + got[:rows, :].astype(F32)).astype(BF16)
    for d, ref in enumerate((g0, g1, g2, g3)):
        at = slice(d * width, (d + 1) * width)
        ref[...] = (mine[rows:, at].astype(F32) + got[rows:, at].astype(F32)).astype(ref.dtype)


def half_loads(side, load, x, wg, wu, xs, ws):
    width = xs.shape[2]
    units = wg.shape[1]
    at = starts(width)[4 * side :]
    return [
        [
            load(x.at[:, pl.ds(d * width, width)], xs.at[d]),
            load(wg.at[pl.ds(at[d], width), :], ws.at[d, :, pl.ds(0, units)]),
            load(wu.at[pl.ds(at[d], width), :], ws.at[d, :, pl.ds(units, units)]),
        ]
        for d in range(4)
    ]


def half_dots(side, copies, ab, xs, ws):
    for d in range(4):
        wait(copies[d])
        term = dot(xs[d], ws[d])
        if d == 0 and side == 0:
            ab[...] = term
        else:
            ab[...] += term


def early_kernel(*refs):
    pieces, (wd, x, wg, wu), (g_ref, ab, cs, vs, xs, ws, sems) = refs[:8], refs[8:12], refs[12:]
    width = cs.shape[2]
    load = Loads(sems)
    copies = [
        [load(pieces[i], cs.at[i]), load(wd.at[:, pl.ds(at, width)], vs.at[i])]
        for i, at in enumerate(starts(width))
    ]
    more = half_loads(0, load, x, wg, wu, xs, ws)
    for i in range(8):
        wait(copies[i])
        term = dot_nt(cs[i], vs[i])
        if i == 0:
            g_ref[...] = term
        else:
            g_ref[...] += term
    half_dots(0, more, ab, xs, ws)


def forth_kernel(x, part, g_ref, wg, wu, wd, a1, a2, a3, oo, hid_ref, dadu_ref, ab, xs, ws, vs, gs, sems):
    width = xs.shape[2]
    units = wg.shape[1]
    load = Loads(sems)
    at = starts(width)
    first = load(part, ab)
    copies = half_loads(1, load, x, wg, wu, xs, ws)
    more = [load(wd.at[:, pl.ds(at[4 + d], width)], vs.at[d]) for d in range(4)]
    copy_g = load(g_ref, gs)
    first.wait()
    half_dots(1, copies, ab, xs, ws)
    act, hidden, slope = gate_terms(ab[:, :units], ab[:, units:])
    copy_g.wait()
    g = gs[...]
    hid_ref[...] = hidden
    dadu_ref[:, :units] = (g * slope).astype(BF16)
    dadu_ref[:, units:] = (g * act).astype(BF16)
    for d in range(4):
        more[d].wait()
        oo[:, d * width : (d + 1) * width] = dot(hidden, vs[d]).astype(BF16)


def cross_kernel(hid_ref, dadu_ref, wg, wu, wd, om, ro, ws, vs, sems):
    width = ws.shape[1]
    units = wg.shape[1]
    load = Loads(sems)
    at = starts(width)
    copies = [
        [
            load(wg.at[pl.ds(at[4 + d], width), :], ws.at[d, :, pl.ds(0, units)]),
            load(wu.at[pl.ds(at[4 + d], width), :], ws.at[d, :, pl.ds(units, units)]),
        ]
        for d in range(4)
    ]
    more = [load(wd.at[:, pl.ds(at[d], width)], vs.at[d]) for d in range(4)]
    for d in range(4):
        wait(copies[d])
        ro[:, d * width : (d + 1) * width] = dot_nt(dadu_ref[...], ws[d]).astype(BF16)
    for d in range(4):
        more[d].wait()
        om[:, d * width : (d + 1) * width] = dot(hid_ref[...], vs[d]).astype(BF16)


def down_kernel(dadu_ref, wg, wu, got, *refs):
    outs, (ws, gs, sems) = refs[:SIDES], refs[SIDES:]
    width = ws.shape[1]
    units = wg.shape[1]
    load = Loads(sems)
    at = starts(width)
    copies = [
        [
            load(wg.at[pl.ds(at[d], width), :], ws.at[d, :, pl.ds(0, units)]),
            load(wu.at[pl.ds(at[d], width), :], ws.at[d, :, pl.ds(units, units)]),
            load(got.at[:, pl.ds(d * width, width)], gs.at[d]),
        ]
        for d in range(SIDES)
    ]
    for d in range(SIDES):
        wait(copies[d])
        outs[d][...] = (dot_nt(dadu_ref[...], ws[d]) + gs[d].astype(F32)).astype(BF16)


def add_kernel(mine, got, out):
    out[...] = (mine[...].astype(F32) + got[...].astype(F32)).astype(BF16)


def sum_kernel(p0, p1, p2, p3, after, out, parts, sems):
    load = Loads(sems)
    copies = [load(p, parts.at[d]) for d, p in enumerate((p0, p1, p2, p3))]
    wait(copies)
    out[...] = (
        parts[0].astype(F32)
        + parts[1].astype(F32)
        + parts[2].astype(F32)
        + parts[3].astype(F32)
    ).astype(BF16)


def mix_kernel(back, pick, gates, dense, pack, *refs):
    outs, inner_ref, (bs, ps, gs, ds, cs, sems) = refs[:SIDES], refs[SIDES], refs[SIDES + 1 :]
    rows, width = outs[0].shape
    load = Loads(sems)
    small = [load(pick, ps), load(gates, gs), load(dense, ds)]
    copies = [
        [
            load(back.at[:, pl.ds(d * width, width)], bs.at[d]),
            load(pack.at[d, pl.ds(rows, rows), :], cs.at[d]),
        ]
        for d in range(SIDES)
    ]
    wait(small)
    gate = [column(gs, k) for k in range(2)]
    inner = [None, None]
    for d in range(SIDES):
        wait(copies[d])
        cotan = cs[d].astype(F32)
        y = dot(ps[...], bs[d])
        total = ds[:, d * width : (d + 1) * width].astype(F32)
        for k in range(2):
            yk = y[k * rows : (k + 1) * rows, :]
            total = total + gate[k] * yk
            term = jnp.sum(cotan * yk, axis=1, keepdims=True)
            inner[k] = term if inner[k] is None else inner[k] + term
        outs[d][...] = total.astype(BF16)
    lane = lax.broadcasted_iota(jnp.int32, (rows, 128), 1)
    inner_ref[...] = jnp.where(lane == 0, inner[0], jnp.where(lane == 1, inner[1], 0.0))


def grad_kernel(back, pick, d0, d1, d2, d3, out):
    rows = out.shape[0]
    z = dot(pick[:rows, :] + pick[rows:, :], back[...])
    dense = d0[...].astype(F32) + d1[...].astype(F32)
    dense = dense + d2[...].astype(F32) + d3[...].astype(F32)
    out[...] = (dense + z).astype(BF16)


def call(kernel, outs, limit, flops, args, name, far_args=(), scratch=(), far_out=False):
    vmem = pl.BlockSpec(memory_space=pltpu.VMEM)
    far = pl.BlockSpec(memory_space=pl.ANY)
    moved = sum(a.size * a.dtype.itemsize for a in args)
    return pl.pallas_call(
        kernel,
        out_shape=[
            pltpu.HBM(*o) if far_out and i == 0 else jax.ShapeDtypeStruct(*o)
            for i, o in enumerate(outs)
        ],
        in_specs=[far if i in far_args else vmem for i in range(len(args))],
        out_specs=[far if far_out and i == 0 else vmem for i in range(len(outs))],
        compiler_params=pltpu.CompilerParams(vmem_limit_bytes=limit * MIB),
        cost_estimate=pl.CostEstimate(flops=flops, bytes_accessed=moved, transcendentals=0),
        scratch_shapes=list(scratch),
        name=name,
    )(*args)


def local(
    tokens,
    cotangent,
    gates,
    routes,
    dense_gate,
    dense_up,
    dense_down,
    expert_gate,
    expert_up,
    expert_down,
):
    devices = lax.axis_size("tensor")
    rows, width = tokens.shape
    experts = lax.axis_size("dp")
    slots = experts * CAPACITY
    half = SIDES * width
    hidden = expert_gate.shape[2]
    dense_hidden = dense_gate.shape[1]

    def along(v, d):
        return lax.ppermute(
            v, "tensor", [(i, (i + 2 * d) % devices) for i in range(devices)]
        )

    def swap(v):
        return lax.ppermute(v, "tensor", [(i, i ^ 1) for i in range(devices)])

    def spread(v):
        return lax.all_to_all(v, "dp", split_axis=0, concat_axis=0, tiled=True)

    def pin(v):
        return pltpu.with_memory_space_constraint(v, pltpu.HBM)

    wg, wu, wd = pin(expert_gate[0]), pin(expert_up[0]), pin(expert_down[0])
    sems = pltpu.SemaphoreType.DMA
    pick, grads_send, both = call(
        plan_kernel,
        [((2 * rows, slots), BF16), ((slots, width), BF16), ((2 * rows, width), BF16)],
        12,
        2 * 2 * rows * slots * width,
        (routes.T, gates.T, tokens, cotangent),
        "plan",
        far_args=range(4),
        scratch=[pltpu.VMEM((2, rows), jnp.int32), pltpu.VMEM((2, rows), F32), sems((4,))],
    )
    own = [both] + [along(both, d) for d in (1, 2, 3)]
    got_grads, own = lax.optimization_barrier((spread(grads_send), own))
    rows_send, pack = call(
        rows_kernel,
        [((slots, half), BF16), ((SIDES, 2 * rows, width), BF16)],
        12,
        2 * rows * slots * half,
        (pick, *own, got_grads),
        "rows",
        far_args=(5,),
        scratch=[pltpu.VMEM((slots, half), BF16), sems((SIDES,))],
        far_out=True,
    )
    got_rows = spread(rows_send)
    grads_own = [got_grads] + [along(got_grads, d) for d in (1, 2, 3)]
    grads_other = [swap(got_grads)]
    dense_m, dense_o = call(
        dense_kernel,
        [((2 * rows, half), BF16)] * 2,
        24,
        12 * rows * dense_hidden * half * 2,
        (pack, swap(pack), pin(dense_gate), pin(dense_up), pin(dense_down)),
        "dense",
        far_args=range(5),
        scratch=[
            pltpu.VMEM((8, 2 * rows, width), BF16),
            pltpu.VMEM((8, width, 2 * dense_hidden), BF16),
            pltpu.VMEM((8, dense_hidden, width), BF16),
            sems((32,)),
        ],
    )
    grads_own[1:], dense_m = lax.optimization_barrier((grads_own[1:], dense_m))
    grads_other += [swap(v) for v in grads_own[1:]]
    dense_out, *dense_part = call(
        dense_sum_kernel,
        [((rows, half), BF16)] + [((rows, width), BF16)] * SIDES,
        12,
        2 * rows * half,
        (dense_m, swap(dense_o)),
        "dense_sum",
    )
    got_rows, _ = lax.optimization_barrier((got_rows, (grads_other, dense_part)))
    rows_other = swap(got_rows)
    dense_got = [dense_part[0]] + [along(dense_part[d], SIDES - d) for d in (1, 2, 3)]
    half_scratch = [pltpu.VMEM((4, slots, width), BF16), pltpu.VMEM((4, width, 2 * hidden), BF16)]
    g, part = call(
        early_kernel,
        [((slots, hidden), F32), ((slots, 2 * hidden), F32)],
        24,
        8 * slots * hidden * half,
        (*[pin(v) for v in (*grads_own, *grads_other)], wd, got_rows, wg, wu),
        "early",
        far_args=range(12),
        scratch=[
            pltpu.VMEM((8, slots, width), BF16),
            pltpu.VMEM((8, hidden, width), BF16),
            *half_scratch,
            sems((28,)),
        ],
    )
    out_o, hid, dadu = call(
        forth_kernel,
        [((slots, half), BF16), ((slots, hidden), BF16), ((slots, 2 * hidden), BF16)],
        24,
        6 * slots * hidden * half,
        (rows_other, part, g, wg, wu, wd, *dense_got[1:]),
        "forth",
        far_args=range(9),
        scratch=[
            pltpu.VMEM((slots, 2 * hidden), F32),
            *half_scratch,
            pltpu.VMEM((4, hidden, width), BF16),
            pltpu.VMEM((slots, hidden), F32),
            sems((18,)),
        ],
    )
    out_got = swap(out_o)
    out_m, grad_o = call(
        cross_kernel,
        [((slots, half), BF16)] * 2,
        20,
        6 * slots * hidden * half,
        (hid, dadu, wg, wu, wd),
        "cross",
        far_args=range(2, 5),
        scratch=[half_scratch[1], pltpu.VMEM((4, hidden, width), BF16), sems((12,))],
    )
    grad_got = swap(grad_o)
    (out_chip,) = call(
        add_kernel,
        [((slots, half), BF16)],
        12,
        slots * half,
        (out_m, out_got),
        "add",
    )
    out_back = spread(out_chip)
    grad_part = call(
        down_kernel,
        [((slots, width), BF16)] * SIDES,
        20,
        4 * slots * hidden * half,
        (dadu, wg, wu, grad_got),
        "down",
        far_args=(1, 2, 3),
        scratch=[half_scratch[1], pltpu.VMEM((SIDES, slots, width), BF16), sems((12,))],
    )
    grad_all = [grad_part[0]] + [along(grad_part[d], SIDES - d) for d in (1, 2, 3)]
    m0, m1, m2, m3, inner = call(
        mix_kernel,
        [((rows, width), BF16)] * 4 + [((rows, 128), F32)],
        16,
        4 * rows * slots * half,
        (out_back, pin(pick), gates.T, pin(dense_out), pin(pack)),
        "mix",
        far_args=range(5),
        scratch=[
            pltpu.VMEM((SIDES, slots, width), BF16),
            pltpu.VMEM((2 * rows, slots), BF16),
            pltpu.VMEM((2, rows), F32),
            pltpu.VMEM((rows, half), BF16),
            pltpu.VMEM((SIDES, rows, width), BF16),
            sems((11,)),
        ],
    )
    (grad_sum,) = call(
        sum_kernel,
        [((slots, width), BF16)],
        12,
        3 * slots * width,
        (*grad_all, inner),
        "sum",
        far_args=range(5),
        scratch=[pltpu.VMEM((SIDES, slots, width), BF16), sems((SIDES,))],
    )
    grad_back = spread(grad_sum)
    mixed = m0.astype(F32)
    for d, part in ((1, m1), (2, m2), (3, m3)):
        mixed = mixed + along(part, SIDES - d).astype(F32)
    inner = inner[:, :2]
    inner = inner + swap(inner)
    gate_grad = inner + along(inner, 1) + along(inner, 2) + along(inner, 3)
    (token_grad,) = call(
        grad_kernel,
        [((rows, width), BF16)],
        12,
        2 * rows * slots * width,
        (grad_back, pick, *dense_got),
        "grad",
    )
    return (mixed.astype(BF16), token_grad, gate_grad)


def solution(mesh):
    in_specs = (
        P("dp", "tensor"),
        P("dp", "tensor"),
        P("dp", None),
        P("dp", None),
        P(None, "tensor"),
        P(None, "tensor"),
        P("tensor", None),
        P("dp", None, "tensor"),
        P("dp", None, "tensor"),
        P("dp", "tensor", None),
    )
    out_specs = (P("dp", "tensor"), P("dp", "tensor"), P("dp", None))
    return jax.shard_map(local, mesh=mesh, in_specs=in_specs, out_specs=out_specs, check_vma=False)
```

```python
import functools

import jax
import jax.numpy as jnp
from jax import lax
from jax.experimental import pallas as pl
from jax.experimental.pallas import tpu as pltpu
from jax.sharding import PartitionSpec as P

F32 = jnp.float32
BF16 = jnp.bfloat16
MIB = 1 << 20
CAPACITY = 32
SIDES = 4


def dot(a, b, contract=((1,), (0,))):
    return lax.dot_general(a, b, (contract, ((), ())), preferred_element_type=F32)


def dot_nt(a, b):
    return dot(a, b, ((1,), (1,)))


def dot_tn(a, b):
    return dot(a, b, ((0,), (0,)))


def gate_terms(a, b):
    s = jax.nn.sigmoid(a)
    act = a * s
    return act, (act * b).astype(BF16), b * s * (1.0 + a * (1.0 - s))


def column(ref, k):
    rows = ref.shape[1]
    eye = lax.broadcasted_iota(jnp.int32, (rows, rows), 0) == lax.broadcasted_iota(
        jnp.int32, (rows, rows), 1
    )
    return jnp.sum(jnp.where(eye, ref[k : k + 1, :].astype(F32), 0.0), axis=1, keepdims=True)


def plan_kernel(routes, gates, tokens, cotangent, pick_ref, send_ref, both_ref, *scratch):
    routes_ref, gates_ref, sems = scratch
    rows = tokens.shape[0]
    slots = pick_ref.shape[1]
    load = Loads(sems)
    first = load(routes, routes_ref)
    copies = [
        load(gates, gates_ref),
        load(cotangent, both_ref.at[pl.ds(rows, rows), :]),
        load(tokens, both_ref.at[pl.ds(0, rows), :]),
    ]
    first.wait()
    lane = lax.broadcasted_iota(jnp.int32, (rows, 128), 1)
    route = [column(routes_ref, k).astype(jnp.int32) for k in range(2)]
    one = [(route[k] == lane).astype(F32) for k in range(2)]
    lower = (
        lax.broadcasted_iota(jnp.int32, (rows, rows), 1)
        < lax.broadcasted_iota(jnp.int32, (rows, rows), 0)
    ).astype(BF16)
    earlier = dot(lower, (one[0] + one[1]).astype(BF16))
    place = lax.broadcasted_iota(jnp.int32, (rows, slots), 1)
    wait(copies)
    cotan = both_ref[rows:, :].astype(F32)
    total = None
    for k in range(2):
        pos = jnp.sum(earlier * one[k], axis=1, keepdims=True).astype(jnp.int32)
        slot = route[k] * CAPACITY + pos
        pick = (slot == place).astype(BF16)
        pick_ref[k * rows : (k + 1) * rows, :] = pick
        scaled = (column(gates_ref, k) * cotan).astype(BF16)
        term = dot_tn(pick, scaled)
        total = term if total is None else total + term
    send_ref[...] = total.astype(BF16)


def rows_kernel(pick_ref, p0, p1, p2, p3, after, send_ref, pack_ref, out, sems):
    rows = p0.shape[0] // 2
    width = p0.shape[1]
    load = Loads(sems)
    pick = pick_ref[:rows, :] + pick_ref[rows:, :]
    copies = []
    for d, piece in enumerate((p0, p1, p2, p3)):
        at = pl.ds(d * width, width)
        out[:, at] = dot_tn(pick, piece[:rows, :]).astype(BF16)
        copies.append(load(out.at[:, at], send_ref.at[:, at]))
        pack_ref[d] = piece[...]
    wait(copies)


def starts(width):
    me = lax.axis_index("tensor")
    chip, core = me // 2, lax.rem(me, 2)
    chips = [lax.rem(chip + SIDES - d, SIDES) for d in range(SIDES)]
    mine = [pl.multiple_of((2 * c + core) * width, width) for c in chips]
    other = [pl.multiple_of((2 * c + 1 - core) * width, width) for c in chips]
    return mine + other


class Loads:
    def __init__(self, sems):
        self.sems = sems
        self.count = 0

    def __call__(self, src, dst):
        copy = pltpu.make_async_copy(src, dst, self.sems.at[self.count])
        copy.start()
        self.count += 1
        return copy


def wait(copies):
    for copy in copies:
        copy.wait()


def dense_kernel(*refs):
    sides, (wg, wu, wd), outs = refs[:2], refs[2:5], refs[5:7]
    xs, ws, vs, sems = refs[7:]
    rows = xs.shape[1] // 2
    width = xs.shape[2]
    units = wg.shape[1]
    load = Loads(sems)
    copies = []
    for i, at in enumerate(starts(width)):
        copies.append(
            [
                load(sides[i // 4].at[i % 4], xs.at[i]),
                load(wg.at[pl.ds(at, width), :], ws.at[i, :, pl.ds(0, units)]),
                load(wu.at[pl.ds(at, width), :], ws.at[i, :, pl.ds(units, units)]),
                load(wd.at[:, pl.ds(at, width)], vs.at[i]),
            ]
        )
    ab = g = None
    for i in range(8):
        wait(copies[i])
        tab = dot(xs[i, :rows, :], ws[i])
        tg = dot_nt(xs[i, rows:, :], vs[i])
        ab, g = (tab, tg) if ab is None else (ab + tab, g + tg)
    act, hidden, slope = gate_terms(ab[:, :units], ab[:, units:])
    dadu = jnp.concatenate([(g * slope).astype(BF16), (g * act).astype(BF16)], axis=1)
    for i in range(8):
        out, d = outs[i // 4], i % 4
        out[:rows, d * width : (d + 1) * width] = dot(hidden, vs[i]).astype(BF16)
        out[rows:, d * width : (d + 1) * width] = dot_nt(dadu, ws[i]).astype(BF16)


def dense_sum_kernel(mine, got, out_ref, g0, g1, g2, g3):
    rows = out_ref.shape[0]
    width = g0.shape[1]
    out_ref[...] = (mine[:rows, :].astype(F32) + got[:rows, :].astype(F32)).astype(BF16)
    for d, ref in enumerate((g0, g1, g2, g3)):
        at = slice(d * width, (d + 1) * width)
        ref[...] = (mine[rows:, at].astype(F32) + got[rows:, at].astype(F32)).astype(ref.dtype)


def half_loads(side, load, x, wg, wu, xs, ws):
    width = xs.shape[2]
    units = wg.shape[1]
    at = starts(width)[4 * side :]
    return [
        [
            load(x.at[:, pl.ds(d * width, width)], xs.at[d]),
            load(wg.at[pl.ds(at[d], width), :], ws.at[d, :, pl.ds(0, units)]),
            load(wu.at[pl.ds(at[d], width), :], ws.at[d, :, pl.ds(units, units)]),
        ]
        for d in range(4)
    ]


def half_dots(side, copies, ab, xs, ws):
    for d in range(4):
        wait(copies[d])
        term = dot(xs[d], ws[d])
        if d == 0 and side == 0:
            ab[...] = term
        else:
            ab[...] += term


def early_kernel(*refs):
    pieces, (wd, x, wg, wu), (g_ref, ab, cs, vs, xs, ws, sems) = refs[:8], refs[8:12], refs[12:]
    width = cs.shape[2]
    load = Loads(sems)
    copies = [
        [load(pieces[i], cs.at[i]), load(wd.at[:, pl.ds(at, width)], vs.at[i])]
        for i, at in enumerate(starts(width))
    ]
    more = half_loads(0, load, x, wg, wu, xs, ws)
    for i in range(8):
        wait(copies[i])
        term = dot_nt(cs[i], vs[i])
        if i == 0:
            g_ref[...] = term
        else:
            g_ref[...] += term
    half_dots(0, more, ab, xs, ws)


def forth_kernel(x, part, g_ref, wg, wu, wd, a1, a2, a3, oo, hid_ref, dadu_ref, ab, xs, ws, vs, gs, sems):
    width = xs.shape[2]
    units = wg.shape[1]
    load = Loads(sems)
    at = starts(width)
    first = load(part, ab)
    copies = half_loads(1, load, x, wg, wu, xs, ws)
    more = [load(wd.at[:, pl.ds(at[4 + d], width)], vs.at[d]) for d in range(4)]
    copy_g = load(g_ref, gs)
    first.wait()
    half_dots(1, copies, ab, xs, ws)
    act, hidden, slope = gate_terms(ab[:, :units], ab[:, units:])
    copy_g.wait()
    g = gs[...]
    hid_ref[...] = hidden
    dadu_ref[:, :units] = (g * slope).astype(BF16)
    dadu_ref[:, units:] = (g * act).astype(BF16)
    for d in range(4):
        more[d].wait()
        oo[:, d * width : (d + 1) * width] = dot(hidden, vs[d]).astype(BF16)


def cross_kernel(hid_ref, dadu_ref, wg, wu, wd, om, ro, ws, vs, sems):
    width = ws.shape[1]
    units = wg.shape[1]
    load = Loads(sems)
    at = starts(width)
    copies = [
        [
            load(wg.at[pl.ds(at[4 + d], width), :], ws.at[d, :, pl.ds(0, units)]),
            load(wu.at[pl.ds(at[4 + d], width), :], ws.at[d, :, pl.ds(units, units)]),
        ]
        for d in range(4)
    ]
    more = [load(wd.at[:, pl.ds(at[d], width)], vs.at[d]) for d in range(4)]
    for d in range(4):
        wait(copies[d])
        ro[:, d * width : (d + 1) * width] = dot_nt(dadu_ref[...], ws[d]).astype(BF16)
    for d in range(4):
        more[d].wait()
        om[:, d * width : (d + 1) * width] = dot(hid_ref[...], vs[d]).astype(BF16)


def down_kernel(dadu_ref, wg, wu, got, *refs):
    outs, (ws, gs, sems) = refs[:SIDES], refs[SIDES:]
    width = ws.shape[1]
    units = wg.shape[1]
    load = Loads(sems)
    at = starts(width)
    copies = [
        [
            load(wg.at[pl.ds(at[d], width), :], ws.at[d, :, pl.ds(0, units)]),
            load(wu.at[pl.ds(at[d], width), :], ws.at[d, :, pl.ds(units, units)]),
            load(got.at[:, pl.ds(d * width, width)], gs.at[d]),
        ]
        for d in range(SIDES)
    ]
    for d in range(SIDES):
        wait(copies[d])
        outs[d][...] = (dot_nt(dadu_ref[...], ws[d]) + gs[d].astype(F32)).astype(BF16)


def add_kernel(mine, got, out):
    out[...] = (mine[...].astype(F32) + got[...].astype(F32)).astype(BF16)


def sum_kernel(p0, p1, p2, p3, after, out, parts, sems):
    load = Loads(sems)
    copies = [load(p, parts.at[d]) for d, p in enumerate((p0, p1, p2, p3))]
    wait(copies)
    out[...] = (
        parts[0].astype(F32)
        + parts[1].astype(F32)
        + parts[2].astype(F32)
        + parts[3].astype(F32)
    ).astype(BF16)


def mix_kernel(back, pick, gates, dense, pack, *refs):
    outs, inner_ref, (bs, ps, gs, ds, cs, sems) = refs[:SIDES], refs[SIDES], refs[SIDES + 1 :]
    rows, width = outs[0].shape
    load = Loads(sems)
    small = [load(pick, ps), load(gates, gs), load(dense, ds)]
    copies = [
        [
            load(back.at[:, pl.ds(d * width, width)], bs.at[d]),
            load(pack.at[d, pl.ds(rows, rows), :], cs.at[d]),
        ]
        for d in range(SIDES)
    ]
    wait(small)
    gate = [column(gs, k) for k in range(2)]
    inner = [None, None]
    for d in range(SIDES):
        wait(copies[d])
        cotan = cs[d].astype(F32)
        y = dot(ps[...], bs[d])
        total = ds[:, d * width : (d + 1) * width].astype(F32)
        for k in range(2):
            yk = y[k * rows : (k + 1) * rows, :]
            total = total + gate[k] * yk
            term = jnp.sum(cotan * yk, axis=1, keepdims=True)
            inner[k] = term if inner[k] is None else inner[k] + term
        outs[d][...] = total.astype(BF16)
    lane = lax.broadcasted_iota(jnp.int32, (rows, 128), 1)
    inner_ref[...] = jnp.where(lane == 0, inner[0], jnp.where(lane == 1, inner[1], 0.0))


def grad_kernel(back, pick, d0, d1, d2, d3, out):
    rows = out.shape[0]
    z = dot(pick[:rows, :] + pick[rows:, :], back[...])
    dense = d0[...].astype(F32) + d1[...].astype(F32)
    dense = dense + d2[...].astype(F32) + d3[...].astype(F32)
    out[...] = (dense + z).astype(BF16)


def call(kernel, outs, limit, flops, args, name, far_args=(), scratch=(), far_out=False):
    vmem = pl.BlockSpec(memory_space=pltpu.VMEM)
    far = pl.BlockSpec(memory_space=pl.ANY)
    moved = sum(a.size * a.dtype.itemsize for a in args)
    return pl.pallas_call(
        kernel,
        out_shape=[
            pltpu.HBM(*o) if far_out and i == 0 else jax.ShapeDtypeStruct(*o)
            for i, o in enumerate(outs)
        ],
        in_specs=[far if i in far_args else vmem for i in range(len(args))],
        out_specs=[far if far_out and i == 0 else vmem for i in range(len(outs))],
        compiler_params=pltpu.CompilerParams(vmem_limit_bytes=limit * MIB),
        cost_estimate=pl.CostEstimate(flops=flops, bytes_accessed=moved, transcendentals=0),
        scratch_shapes=list(scratch),
        name=name,
    )(*args)


def local(
    tokens,
    cotangent,
    gates,
    routes,
    dense_gate,
    dense_up,
    dense_down,
    expert_gate,
    expert_up,
    expert_down,
):
    devices = lax.axis_size("tensor")
    rows, width = tokens.shape
    experts = lax.axis_size("dp")
    slots = experts * CAPACITY
    half = SIDES * width
    hidden = expert_gate.shape[2]
    dense_hidden = dense_gate.shape[1]

    def along(v, d):
        return lax.ppermute(
            v, "tensor", [(i, (i + 2 * d) % devices) for i in range(devices)]
        )

    def swap(v):
        return lax.ppermute(v, "tensor", [(i, i ^ 1) for i in range(devices)])

    def spread(v):
        return lax.all_to_all(v, "dp", split_axis=0, concat_axis=0, tiled=True)

    def pin(v):
        return pltpu.with_memory_space_constraint(v, pltpu.HBM)

    wg, wu, wd = pin(expert_gate[0]), pin(expert_up[0]), pin(expert_down[0])
    sems = pltpu.SemaphoreType.DMA
    pick, grads_send, both = call(
        plan_kernel,
        [((2 * rows, slots), BF16), ((slots, width), BF16), ((2 * rows, width), BF16)],
        12,
        2 * 2 * rows * slots * width,
        (pin(routes.T), pin(gates.T), pin(tokens), pin(cotangent)),
        "plan",
        far_args=range(4),
        scratch=[pltpu.VMEM((2, rows), jnp.int32), pltpu.VMEM((2, rows), F32), sems((4,))],
    )
    own = [both] + [along(both, d) for d in (1, 2, 3)]
    got_grads, own = lax.optimization_barrier((spread(grads_send), own))
    rows_send, pack = call(
        rows_kernel,
        [((slots, half), BF16), ((SIDES, 2 * rows, width), BF16)],
        12,
        2 * rows * slots * half,
        (pick, *own, got_grads),
        "rows",
        far_args=(5,),
        scratch=[pltpu.VMEM((slots, half), BF16), sems((SIDES,))],
        far_out=True,
    )
    got_rows = spread(rows_send)
    grads_own = [got_grads] + [along(got_grads, d) for d in (1, 2, 3)]
    grads_other = [swap(got_grads)]
    dense_m, dense_o = call(
        dense_kernel,
        [((2 * rows, half), BF16)] * 2,
        24,
        12 * rows * dense_hidden * half * 2,
        (pack, swap(pack), pin(dense_gate), pin(dense_up), pin(dense_down)),
        "dense",
        far_args=range(5),
        scratch=[
            pltpu.VMEM((8, 2 * rows, width), BF16),
            pltpu.VMEM((8, width, 2 * dense_hidden), BF16),
            pltpu.VMEM((8, dense_hidden, width), BF16),
            sems((32,)),
        ],
    )
    grads_own[1:], dense_m = lax.optimization_barrier((grads_own[1:], dense_m))
    grads_other += [swap(v) for v in grads_own[1:]]
    dense_out, *dense_part = call(
        dense_sum_kernel,
        [((rows, half), BF16)] + [((rows, width), BF16)] * SIDES,
        12,
        2 * rows * half,
        (dense_m, swap(dense_o)),
        "dense_sum",
    )
    got_rows, _ = lax.optimization_barrier((got_rows, (grads_other, dense_part)))
    rows_other = swap(got_rows)
    dense_got = [dense_part[0]] + [along(dense_part[d], SIDES - d) for d in (1, 2, 3)]
    half_scratch = [pltpu.VMEM((4, slots, width), BF16), pltpu.VMEM((4, width, 2 * hidden), BF16)]
    g, part = call(
        early_kernel,
        [((slots, hidden), F32), ((slots, 2 * hidden), F32)],
        24,
        8 * slots * hidden * half,
        (*[pin(v) for v in (*grads_own, *grads_other)], wd, got_rows, wg, wu),
        "early",
        far_args=range(12),
        scratch=[
            pltpu.VMEM((8, slots, width), BF16),
            pltpu.VMEM((8, hidden, width), BF16),
            *half_scratch,
            sems((28,)),
        ],
    )
    out_o, hid, dadu = call(
        forth_kernel,
        [((slots, half), BF16), ((slots, hidden), BF16), ((slots, 2 * hidden), BF16)],
        24,
        6 * slots * hidden * half,
        (rows_other, part, g, wg, wu, wd, *dense_got[1:]),
        "forth",
        far_args=range(9),
        scratch=[
            pltpu.VMEM((slots, 2 * hidden), F32),
            *half_scratch,
            pltpu.VMEM((4, hidden, width), BF16),
            pltpu.VMEM((slots, hidden), F32),
            sems((18,)),
        ],
    )
    out_got = swap(out_o)
    out_m, grad_o = call(
        cross_kernel,
        [((slots, half), BF16)] * 2,
        20,
        6 * slots * hidden * half,
        (hid, dadu, wg, wu, wd),
        "cross",
        far_args=range(2, 5),
        scratch=[half_scratch[1], pltpu.VMEM((4, hidden, width), BF16), sems((12,))],
    )
    grad_got = swap(grad_o)
    (out_chip,) = call(
        add_kernel,
        [((slots, half), BF16)],
        12,
        slots * half,
        (out_m, out_got),
        "add",
    )
    out_back = spread(out_chip)
    grad_part = call(
        down_kernel,
        [((slots, width), BF16)] * SIDES,
        20,
        4 * slots * hidden * half,
        (dadu, wg, wu, grad_got),
        "down",
        far_args=(1, 2, 3),
        scratch=[half_scratch[1], pltpu.VMEM((SIDES, slots, width), BF16), sems((12,))],
    )
    grad_all = [grad_part[0]] + [along(grad_part[d], SIDES - d) for d in (1, 2, 3)]
    m0, m1, m2, m3, inner = call(
        mix_kernel,
        [((rows, width), BF16)] * 4 + [((rows, 128), F32)],
        16,
        4 * rows * slots * half,
        (out_back, pin(pick), gates.T, pin(dense_out), pin(pack)),
        "mix",
        far_args=range(5),
        scratch=[
            pltpu.VMEM((SIDES, slots, width), BF16),
            pltpu.VMEM((2 * rows, slots), BF16),
            pltpu.VMEM((2, rows), F32),
            pltpu.VMEM((rows, half), BF16),
            pltpu.VMEM((SIDES, rows, width), BF16),
            sems((11,)),
        ],
    )
    (grad_sum,) = call(
        sum_kernel,
        [((slots, width), BF16)],
        12,
        3 * slots * width,
        (*grad_all, inner),
        "sum",
        far_args=range(5),
        scratch=[pltpu.VMEM((SIDES, slots, width), BF16), sems((SIDES,))],
    )
    grad_back = spread(grad_sum)
    mixed = m0.astype(F32)
    for d, part in ((1, m1), (2, m2), (3, m3)):
        mixed = mixed + along(part, SIDES - d).astype(F32)
    inner = inner[:, :2]
    inner = inner + swap(inner)
    gate_grad = inner + along(inner, 1) + along(inner, 2) + along(inner, 3)
    (token_grad,) = call(
        grad_kernel,
        [((rows, width), BF16)],
        12,
        2 * rows * slots * width,
        (grad_back, pick, *dense_got),
        "grad",
    )
    return (mixed.astype(BF16), token_grad, gate_grad)


def solution(mesh):
    in_specs = (
        P("dp", "tensor"),
        P("dp", "tensor"),
        P("dp", None),
        P("dp", None),
        P(None, "tensor"),
        P(None, "tensor"),
        P("tensor", None),
        P("dp", None, "tensor"),
        P("dp", None, "tensor"),
        P("dp", "tensor", None),
    )
    out_specs = (P("dp", "tensor"), P("dp", "tensor"), P("dp", None))
    return jax.shard_map(local, mesh=mesh, in_specs=in_specs, out_specs=out_specs, check_vma=False)
```

```python
import functools

import jax
import jax.numpy as jnp
from jax import lax
from jax.experimental import pallas as pl
from jax.experimental.pallas import tpu as pltpu
from jax.sharding import PartitionSpec as P

F32 = jnp.float32
BF16 = jnp.bfloat16
MIB = 1 << 20
CAPACITY = 32
SIDES = 4


def dot(a, b, contract=((1,), (0,))):
    return lax.dot_general(a, b, (contract, ((), ())), preferred_element_type=F32)


def dot_nt(a, b):
    return dot(a, b, ((1,), (1,)))


def dot_tn(a, b):
    return dot(a, b, ((0,), (0,)))


def gate_terms(a, b):
    s = jax.nn.sigmoid(a)
    act = a * s
    return act, (act * b).astype(BF16), b * s * (1.0 + a * (1.0 - s))


def column(ref, k):
    rows = ref.shape[1]
    eye = lax.broadcasted_iota(jnp.int32, (rows, rows), 0) == lax.broadcasted_iota(
        jnp.int32, (rows, rows), 1
    )
    return jnp.sum(jnp.where(eye, ref[k : k + 1, :].astype(F32), 0.0), axis=1, keepdims=True)


def plan_kernel(routes, gates, tokens, cotangent, pick_ref, send_ref, both_ref, *scratch):
    routes_ref, gates_ref, sems = scratch
    rows = tokens.shape[0]
    slots = pick_ref.shape[1]
    load = Loads(sems)
    first = load(routes, routes_ref)
    copies = [
        load(gates, gates_ref),
        load(cotangent, both_ref.at[pl.ds(rows, rows), :]),
        load(tokens, both_ref.at[pl.ds(0, rows), :]),
    ]
    first.wait()
    lane = lax.broadcasted_iota(jnp.int32, (rows, 128), 1)
    route = [column(routes_ref, k).astype(jnp.int32) for k in range(2)]
    one = [(route[k] == lane).astype(F32) for k in range(2)]
    lower = (
        lax.broadcasted_iota(jnp.int32, (rows, rows), 1)
        < lax.broadcasted_iota(jnp.int32, (rows, rows), 0)
    ).astype(BF16)
    earlier = dot(lower, (one[0] + one[1]).astype(BF16))
    place = lax.broadcasted_iota(jnp.int32, (rows, slots), 1)
    wait(copies)
    cotan = both_ref[rows:, :].astype(F32)
    total = None
    for k in range(2):
        pos = jnp.sum(earlier * one[k], axis=1, keepdims=True).astype(jnp.int32)
        slot = route[k] * CAPACITY + pos
        pick = (slot == place).astype(BF16)
        pick_ref[k * rows : (k + 1) * rows, :] = pick
        scaled = (column(gates_ref, k) * cotan).astype(BF16)
        term = dot_tn(pick, scaled)
        total = term if total is None else total + term
    send_ref[...] = total.astype(BF16)


def rows_kernel(pick_ref, p0, p1, p2, p3, after, send_ref, pack_ref, out, sems):
    rows = p0.shape[0] // 2
    width = p0.shape[1]
    load = Loads(sems)
    pick = pick_ref[:rows, :] + pick_ref[rows:, :]
    copies = []
    for d, piece in enumerate((p0, p1, p2, p3)):
        at = pl.ds(d * width, width)
        out[:, at] = dot_tn(pick, piece[:rows, :]).astype(BF16)
        copies.append(load(out.at[:, at], send_ref.at[:, at]))
        pack_ref[d] = piece[...]
    wait(copies)


def starts(width):
    me = lax.axis_index("tensor")
    chip, core = me // 2, lax.rem(me, 2)
    chips = [lax.rem(chip + SIDES - d, SIDES) for d in range(SIDES)]
    mine = [pl.multiple_of((2 * c + core) * width, width) for c in chips]
    other = [pl.multiple_of((2 * c + 1 - core) * width, width) for c in chips]
    return mine + other


class Loads:
    def __init__(self, sems):
        self.sems = sems
        self.count = 0

    def __call__(self, src, dst):
        copy = pltpu.make_async_copy(src, dst, self.sems.at[self.count])
        copy.start()
        self.count += 1
        return copy


def wait(copies):
    for copy in copies:
        copy.wait()


def dense_kernel(*refs):
    sides, (wg, wu, wd), outs = refs[:2], refs[2:5], refs[5:7]
    xs, ws, vs, sems = refs[7:]
    rows = xs.shape[1] // 2
    width = xs.shape[2]
    units = wg.shape[1]
    load = Loads(sems)
    copies = []
    for i, at in enumerate(starts(width)):
        copies.append(
            [
                load(sides[i // 4].at[i % 4], xs.at[i]),
                load(wg.at[pl.ds(at, width), :], ws.at[i, :, pl.ds(0, units)]),
                load(wu.at[pl.ds(at, width), :], ws.at[i, :, pl.ds(units, units)]),
                load(wd.at[:, pl.ds(at, width)], vs.at[i]),
            ]
        )
    ab = g = None
    for i in range(8):
        wait(copies[i])
        tab = dot(xs[i, :rows, :], ws[i])
        tg = dot_nt(xs[i, rows:, :], vs[i])
        ab, g = (tab, tg) if ab is None else (ab + tab, g + tg)
    act, hidden, slope = gate_terms(ab[:, :units], ab[:, units:])
    dadu = jnp.concatenate([(g * slope).astype(BF16), (g * act).astype(BF16)], axis=1)
    for i in range(8):
        out, d = outs[i // 4], i % 4
        out[:rows, d * width : (d + 1) * width] = dot(hidden, vs[i]).astype(BF16)
        out[rows:, d * width : (d + 1) * width] = dot_nt(dadu, ws[i]).astype(BF16)


def dense_sum_kernel(mine, got, out_ref, g0, g1, g2, g3):
    rows = out_ref.shape[0]
    width = g0.shape[1]
    out_ref[...] = (mine[:rows, :].astype(F32) + got[:rows, :].astype(F32)).astype(BF16)
    for d, ref in enumerate((g0, g1, g2, g3)):
        at = slice(d * width, (d + 1) * width)
        ref[...] = (mine[rows:, at].astype(F32) + got[rows:, at].astype(F32)).astype(ref.dtype)


def half_loads(side, load, x, wg, wu, xs, ws):
    width = xs.shape[2]
    units = wg.shape[1]
    at = starts(width)[4 * side :]
    return [
        [
            load(x.at[:, pl.ds(d * width, width)], xs.at[d]),
            load(wg.at[pl.ds(at[d], width), :], ws.at[d, :, pl.ds(0, units)]),
            load(wu.at[pl.ds(at[d], width), :], ws.at[d, :, pl.ds(units, units)]),
        ]
        for d in range(4)
    ]


def half_dots(side, copies, ab, xs, ws):
    for d in range(4):
        wait(copies[d])
        term = dot(xs[d], ws[d])
        if d == 0 and side == 0:
            ab[...] = term
        else:
            ab[...] += term


def early_kernel(*refs):
    pieces, (wd, x, wg, wu), (g_ref, ab, cs, vs, xs, ws, sems) = refs[:8], refs[8:12], refs[12:]
    width = cs.shape[2]
    load = Loads(sems)
    copies = [
        [load(pieces[i], cs.at[i]), load(wd.at[:, pl.ds(at, width)], vs.at[i])]
        for i, at in enumerate(starts(width))
    ]
    more = half_loads(0, load, x, wg, wu, xs, ws)
    for i in range(8):
        wait(copies[i])
        term = dot_nt(cs[i], vs[i])
        if i == 0:
            g_ref[...] = term
        else:
            g_ref[...] += term
    half_dots(0, more, ab, xs, ws)


def forth_kernel(x, part, g_ref, wg, wu, wd, a1, a2, a3, oo, hid_ref, dadu_ref, ab, xs, ws, vs, gs, sems):
    width = xs.shape[2]
    units = wg.shape[1]
    load = Loads(sems)
    at = starts(width)
    first = load(part, ab)
    copies = half_loads(1, load, x, wg, wu, xs, ws)
    more = [load(wd.at[:, pl.ds(at[4 + d], width)], vs.at[d]) for d in range(4)]
    copy_g = load(g_ref, gs)
    first.wait()
    half_dots(1, copies, ab, xs, ws)
    act, hidden, slope = gate_terms(ab[:, :units], ab[:, units:])
    copy_g.wait()
    g = gs[...]
    hid_ref[...] = hidden
    dadu_ref[:, :units] = (g * slope).astype(BF16)
    dadu_ref[:, units:] = (g * act).astype(BF16)
    for d in range(4):
        more[d].wait()
        oo[:, d * width : (d + 1) * width] = dot(hidden, vs[d]).astype(BF16)


def cross_kernel(hid_ref, dadu_ref, wg, wu, wd, om, ro, ws, vs, sems):
    width = ws.shape[1]
    units = wg.shape[1]
    load = Loads(sems)
    at = starts(width)
    copies = [
        [
            load(wg.at[pl.ds(at[4 + d], width), :], ws.at[d, :, pl.ds(0, units)]),
            load(wu.at[pl.ds(at[4 + d], width), :], ws.at[d, :, pl.ds(units, units)]),
        ]
        for d in range(4)
    ]
    more = [load(wd.at[:, pl.ds(at[d], width)], vs.at[d]) for d in range(4)]
    for d in range(4):
        wait(copies[d])
        ro[:, d * width : (d + 1) * width] = dot_nt(dadu_ref[...], ws[d]).astype(BF16)
    for d in range(4):
        more[d].wait()
        om[:, d * width : (d + 1) * width] = dot(hid_ref[...], vs[d]).astype(BF16)


def down_kernel(dadu_ref, wg, wu, got, *refs):
    outs, (ws, gs, sems) = refs[:SIDES], refs[SIDES:]
    width = ws.shape[1]
    sent = []
    units = wg.shape[1]
    load = Loads(sems)
    at = starts(width)
    copies = [
        [
            load(wg.at[pl.ds(at[d], width), :], ws.at[d, :, pl.ds(0, units)]),
            load(wu.at[pl.ds(at[d], width), :], ws.at[d, :, pl.ds(units, units)]),
            load(got.at[:, pl.ds(d * width, width)], gs.at[d]),
        ]
        for d in range(SIDES)
    ]
    for d in range(SIDES):
        wait(copies[d])
        gs[d] = (dot_nt(dadu_ref[...], ws[d]) + gs[d].astype(F32)).astype(BF16)
        sent.append(load(gs.at[d], outs[d]))
    wait(sent)


def add_kernel(mine, got, out):
    out[...] = (mine[...].astype(F32) + got[...].astype(F32)).astype(BF16)


def sum_kernel(p0, p1, p2, p3, after, out, parts, sems):
    load = Loads(sems)
    copies = [load(p, parts.at[d]) for d, p in enumerate((p0, p1, p2, p3))]
    wait(copies)
    out[...] = (
        parts[0].astype(F32)
        + parts[1].astype(F32)
        + parts[2].astype(F32)
        + parts[3].astype(F32)
    ).astype(BF16)


def mix_kernel(back, pick, gates, dense, pack, *refs):
    outs, inner_ref, (bs, ps, gs, ds, cs, sems) = refs[:SIDES], refs[SIDES], refs[SIDES + 1 :]
    rows, width = outs[0].shape
    load = Loads(sems)
    small = [load(pick, ps), load(gates, gs), load(dense, ds)]
    copies = [
        [
            load(back.at[:, pl.ds(d * width, width)], bs.at[d]),
            load(pack.at[d, pl.ds(rows, rows), :], cs.at[d]),
        ]
        for d in range(SIDES)
    ]
    wait(small)
    gate = [column(gs, k) for k in range(2)]
    inner = [None, None]
    for d in range(SIDES):
        wait(copies[d])
        cotan = cs[d].astype(F32)
        y = dot(ps[...], bs[d])
        total = ds[:, d * width : (d + 1) * width].astype(F32)
        for k in range(2):
            yk = y[k * rows : (k + 1) * rows, :]
            total = total + gate[k] * yk
            term = jnp.sum(cotan * yk, axis=1, keepdims=True)
            inner[k] = term if inner[k] is None else inner[k] + term
        outs[d][...] = total.astype(BF16)
    lane = lax.broadcasted_iota(jnp.int32, (rows, 128), 1)
    inner_ref[...] = jnp.where(lane == 0, inner[0], jnp.where(lane == 1, inner[1], 0.0))


def grad_kernel(back, pick, d0, d1, d2, d3, out):
    rows = out.shape[0]
    z = dot(pick[:rows, :] + pick[rows:, :], back[...])
    dense = d0[...].astype(F32) + d1[...].astype(F32)
    dense = dense + d2[...].astype(F32) + d3[...].astype(F32)
    out[...] = (dense + z).astype(BF16)


def call(kernel, outs, limit, flops, args, name, far_args=(), scratch=(), far_out=0):
    vmem = pl.BlockSpec(memory_space=pltpu.VMEM)
    far = pl.BlockSpec(memory_space=pl.ANY)
    moved = sum(a.size * a.dtype.itemsize for a in args)
    return pl.pallas_call(
        kernel,
        out_shape=[
            pltpu.HBM(*o) if i < far_out else jax.ShapeDtypeStruct(*o)
            for i, o in enumerate(outs)
        ],
        in_specs=[far if i in far_args else vmem for i in range(len(args))],
        out_specs=[far if i < far_out else vmem for i in range(len(outs))],
        compiler_params=pltpu.CompilerParams(vmem_limit_bytes=limit * MIB),
        cost_estimate=pl.CostEstimate(flops=flops, bytes_accessed=moved, transcendentals=0),
        scratch_shapes=list(scratch),
        name=name,
    )(*args)


def local(
    tokens,
    cotangent,
    gates,
    routes,
    dense_gate,
    dense_up,
    dense_down,
    expert_gate,
    expert_up,
    expert_down,
):
    devices = lax.axis_size("tensor")
    rows, width = tokens.shape
    experts = lax.axis_size("dp")
    slots = experts * CAPACITY
    half = SIDES * width
    hidden = expert_gate.shape[2]
    dense_hidden = dense_gate.shape[1]

    def along(v, d):
        return lax.ppermute(
            v, "tensor", [(i, (i + 2 * d) % devices) for i in range(devices)]
        )

    def swap(v):
        return lax.ppermute(v, "tensor", [(i, i ^ 1) for i in range(devices)])

    def spread(v):
        return lax.all_to_all(v, "dp", split_axis=0, concat_axis=0, tiled=True)

    def pin(v):
        return pltpu.with_memory_space_constraint(v, pltpu.HBM)

    wg, wu, wd = pin(expert_gate[0]), pin(expert_up[0]), pin(expert_down[0])
    sems = pltpu.SemaphoreType.DMA
    pick, grads_send, both = call(
        plan_kernel,
        [((2 * rows, slots), BF16), ((slots, width), BF16), ((2 * rows, width), BF16)],
        12,
        2 * 2 * rows * slots * width,
        (pin(routes.T), pin(gates.T), pin(tokens), pin(cotangent)),
        "plan",
        far_args=range(4),
        scratch=[pltpu.VMEM((2, rows), jnp.int32), pltpu.VMEM((2, rows), F32), sems((4,))],
    )
    own = [both] + [along(both, d) for d in (1, 2, 3)]
    got_grads, own = lax.optimization_barrier((spread(grads_send), own))
    rows_send, pack = call(
        rows_kernel,
        [((slots, half), BF16), ((SIDES, 2 * rows, width), BF16)],
        12,
        2 * rows * slots * half,
        (pick, *own, got_grads),
        "rows",
        far_args=(5,),
        scratch=[pltpu.VMEM((slots, half), BF16), sems((SIDES,))],
        far_out=1,
    )
    got_rows = spread(rows_send)
    grads_own = [got_grads] + [along(got_grads, d) for d in (1, 2, 3)]
    grads_other = [swap(got_grads)]
    dense_m, dense_o = call(
        dense_kernel,
        [((2 * rows, half), BF16)] * 2,
        24,
        12 * rows * dense_hidden * half * 2,
        (pack, swap(pack), pin(dense_gate), pin(dense_up), pin(dense_down)),
        "dense",
        far_args=range(5),
        scratch=[
            pltpu.VMEM((8, 2 * rows, width), BF16),
            pltpu.VMEM((8, width, 2 * dense_hidden), BF16),
            pltpu.VMEM((8, dense_hidden, width), BF16),
            sems((32,)),
        ],
    )
    grads_own[1:], dense_m = lax.optimization_barrier((grads_own[1:], dense_m))
    grads_other += [swap(v) for v in grads_own[1:]]
    dense_out, *dense_part = call(
        dense_sum_kernel,
        [((rows, half), BF16)] + [((rows, width), BF16)] * SIDES,
        12,
        2 * rows * half,
        (dense_m, swap(dense_o)),
        "dense_sum",
    )
    got_rows, _ = lax.optimization_barrier((got_rows, (grads_other, dense_part)))
    rows_other = swap(got_rows)
    dense_got = [dense_part[0]] + [along(dense_part[d], SIDES - d) for d in (1, 2, 3)]
    half_scratch = [pltpu.VMEM((4, slots, width), BF16), pltpu.VMEM((4, width, 2 * hidden), BF16)]
    g, part = call(
        early_kernel,
        [((slots, hidden), F32), ((slots, 2 * hidden), F32)],
        24,
        8 * slots * hidden * half,
        (*[pin(v) for v in (*grads_own, *grads_other)], wd, got_rows, wg, wu),
        "early",
        far_args=range(12),
        scratch=[
            pltpu.VMEM((8, slots, width), BF16),
            pltpu.VMEM((8, hidden, width), BF16),
            *half_scratch,
            sems((28,)),
        ],
    )
    out_o, hid, dadu = call(
        forth_kernel,
        [((slots, half), BF16), ((slots, hidden), BF16), ((slots, 2 * hidden), BF16)],
        24,
        6 * slots * hidden * half,
        (rows_other, part, g, wg, wu, wd, *dense_got[1:]),
        "forth",
        far_args=range(9),
        scratch=[
            pltpu.VMEM((slots, 2 * hidden), F32),
            *half_scratch,
            pltpu.VMEM((4, hidden, width), BF16),
            pltpu.VMEM((slots, hidden), F32),
            sems((18,)),
        ],
    )
    out_got = swap(out_o)
    out_m, grad_o = call(
        cross_kernel,
        [((slots, half), BF16)] * 2,
        20,
        6 * slots * hidden * half,
        (hid, dadu, wg, wu, wd),
        "cross",
        far_args=range(2, 5),
        scratch=[half_scratch[1], pltpu.VMEM((4, hidden, width), BF16), sems((12,))],
    )
    grad_got = swap(grad_o)
    (out_chip,) = call(
        add_kernel,
        [((slots, half), BF16)],
        12,
        slots * half,
        (out_m, out_got),
        "add",
    )
    out_back = spread(out_chip)
    grad_part = call(
        down_kernel,
        [((slots, width), BF16)] * SIDES,
        20,
        4 * slots * hidden * half,
        (dadu, wg, wu, grad_got),
        "down",
        far_args=(1, 2, 3),
        scratch=[half_scratch[1], pltpu.VMEM((SIDES, slots, width), BF16), sems((16,))],
        far_out=SIDES,
    )
    grad_all = [grad_part[0]] + [along(grad_part[d], SIDES - d) for d in (1, 2, 3)]
    m0, m1, m2, m3, inner = call(
        mix_kernel,
        [((rows, width), BF16)] * 4 + [((rows, 128), F32)],
        16,
        4 * rows * slots * half,
        (out_back, pin(pick), gates.T, pin(dense_out), pin(pack)),
        "mix",
        far_args=range(5),
        scratch=[
            pltpu.VMEM((SIDES, slots, width), BF16),
            pltpu.VMEM((2 * rows, slots), BF16),
            pltpu.VMEM((2, rows), F32),
            pltpu.VMEM((rows, half), BF16),
            pltpu.VMEM((SIDES, rows, width), BF16),
            sems((11,)),
        ],
    )
    (grad_sum,) = call(
        sum_kernel,
        [((slots, width), BF16)],
        12,
        3 * slots * width,
        (*grad_all, inner),
        "sum",
        far_args=range(5),
        scratch=[pltpu.VMEM((SIDES, slots, width), BF16), sems((SIDES,))],
    )
    grad_back = spread(grad_sum)
    mixed = m0.astype(F32)
    for d, part in ((1, m1), (2, m2), (3, m3)):
        mixed = mixed + along(part, SIDES - d).astype(F32)
    inner = inner[:, :2]
    inner = inner + swap(inner)
    gate_grad = inner + along(inner, 1) + along(inner, 2) + along(inner, 3)
    (token_grad,) = call(
        grad_kernel,
        [((rows, width), BF16)],
        12,
        2 * rows * slots * width,
        (grad_back, pick, *dense_got),
        "grad",
    )
    return (mixed.astype(BF16), token_grad, gate_grad)


def solution(mesh):
    in_specs = (
        P("dp", "tensor"),
        P("dp", "tensor"),
        P("dp", None),
        P("dp", None),
        P(None, "tensor"),
        P(None, "tensor"),
        P("tensor", None),
        P("dp", None, "tensor"),
        P("dp", None, "tensor"),
        P("dp", "tensor", None),
    )
    out_specs = (P("dp", "tensor"), P("dp", "tensor"), P("dp", None))
    return jax.shard_map(local, mesh=mesh, in_specs=in_specs, out_specs=out_specs, check_vma=False)
```
